256 devices in a mesh: grid: 32 (over z, y_lo, core), band: 8 (over y_hi, x).
Axes of the slice: x: 4, y: 4 (y_hi: 2, y_lo: 2; y = y_hi * 2 + y_lo), z: 8, core: 2. Of those that a mesh axis runs over, the one named last changes fastest.
Arguments:
- orbitals: float32 [32, 96, 9216], P('band', 'grid'), may hold values from -6 to 6
- sign_vectors: int32 [64, 96, 9216], P('band', 'grid'), may hold values from -1 to 1, as said below
- potential: float32 [96, 9216], P('grid'), may hold values from -0.45 to 0.45
- cheb_coefs: float32 [7], replicated, may hold values from 0.2 to 1
Outputs:
- density: float32 [96, 9216], P('grid', 'band')
- margins: float32 [32, 64], P(None, 'band')
- noise_out: float32 [64, 96, 9216], P('band', 'grid')
The draws below stay inside these ranges and needn't reach their ends.
Inputs may be any that keep to these rules, and one draw needn't show every extreme that they name: `sign_vectors`: every entry is -1 or 1.
All inputs are finite; a program needn't handle non-finite values.
Results may differ from the reference program's by a relative error of at most 0.00012.
Values sent between devices are 32-bit elements; how exact they have to be, the bound alone decides.
A program may use at most 64 MiB of HBM per device.

```python
import math
import jax
import jax.numpy as jnp
from jax import lax

NG = 96
ORB_DEV = 4
STO_DEV = 8
ORDER = 6
NYZ = 9216
ORBITALS = 32
STOCHASTIC = 64
N_BAND = 8


def draw_sign_vectors(key, part):
    key = jax.random.fold_in(key, 11)
    coins = jax.random.randint(key, (STOCHASTIC, NG, NYZ), 0, 2)
    return (2 * coins - 1).astype(jnp.int32)


def level_of(stream_key, extent, pieces, smallest, high):
    loudness = 1.0
    for axis_at, blocks in pieces:
        draws = jax.random.uniform(jax.random.fold_in(jax.random.fold_in(stream_key, 6), axis_at), (blocks,), jnp.float32, smallest / len(pieces), high / len(pieces))
        loudness = loudness * jnp.repeat(jnp.exp(draws), extent[axis_at] // blocks).reshape((-1,) + (1,) * (len(extent) - 1 - axis_at))
    return loudness


def bell_draw(rng, shape, scale, limit, split=(), held_as=jnp.bfloat16):
    level = level_of(rng, shape, split, -0.22, 0.18) if split else 1.0
    result = jax.random.normal(rng, shape, jnp.float32) * scale * level
    return jnp.minimum(jnp.maximum(result, -limit), limit).astype(held_as)


def setup_inputs(seed: int = 0) -> dict:
    arg_keys = jax.random.split(jax.random.key(seed), 5)
    return {
        "orbitals": bell_draw(arg_keys[0], (ORBITALS, NG, NYZ), 1.0, 6.0, ((0, 8), (1, 32)), jnp.float32),
        "sign_vectors": draw_sign_vectors(jax.random.fold_in(arg_keys[4], 71), 0),
        "potential": jnp.clip(jax.random.uniform(arg_keys[2], (NG, NYZ), jnp.float32, -0.45, 0.45) * level_of(arg_keys[2], (NG, NYZ), ((0, 32),), -0.4, 0.0), -0.45, 0.45),
        "cheb_coefs": jnp.clip(jax.random.uniform(arg_keys[3], (ORDER + 1,), jnp.float32, 0.2, 1.0), 0.2, 1.0),
    }


def kinetic_matrix():
    indices = jnp.arange(NG, dtype=jnp.int32)
    product_mod = indices[:, None] * indices[None, :] % NG
    phases = 2.0 * math.pi / NG * product_mod.astype(jnp.float32)
    hartley = (jnp.cos(phases) + jnp.sin(phases)) / math.sqrt(NG)
    wavenumber = jnp.minimum(indices, NG - indices).astype(jnp.float32) / (NG / 2.0)
    spectrum = (wavenumber * wavenumber - 0.5) / 3.0
    return jnp.dot(hartley, spectrum[:, None] * hartley, precision=lax.Precision.HIGHEST)

def apply_operator(current, field_slab, kinetic):
    high = lax.Precision.HIGHEST
    along_x = jnp.einsum('gxyz,wx->gwyz', current, kinetic, precision=high)
    along_y = jnp.einsum('gxyz,wy->gxwz', current, kinetic, precision=high)
    along_z = jnp.einsum('gxyz,wz->gxyw', current, kinetic, precision=high)
    return along_x + along_y + along_z + field_slab[None] * current

def chebyshev(vectors, field_slab, kinetic, cheb_coefs):
    previous = vectors
    current = apply_operator(vectors, field_slab, kinetic)
    filtered = cheb_coefs[0] * previous + cheb_coefs[1] * current
    for order_index in range(2, ORDER + 1):
        following = 2.0 * apply_operator(current, field_slab, kinetic) - previous
        filtered = filtered + cheb_coefs[order_index] * following
        previous, current = (current, following)
    return filtered

def reference(orbitals, sign_vectors, potential, cheb_coefs):
    high = lax.Precision.HIGHEST
    kinetic = kinetic_matrix()
    scale_root = math.sqrt(float(NG) ** 3)
    noise = sign_vectors.astype(jnp.float32)
    flat_orbitals = orbitals.reshape(ORBITALS, NG * NYZ)
    flat_noise = noise.reshape(STOCHASTIC, NG * NYZ)
    margins = jnp.einsum('in,sn->is', flat_orbitals, flat_noise, precision=high) / scale_root
    projected = flat_noise - jnp.einsum('is,in->sn', margins, flat_orbitals, precision=high) / scale_root
    field_slab = potential.reshape(NG, NG, NG)
    joined = jnp.concatenate([flat_orbitals, projected], 0)
    groups = joined.reshape(N_BAND, ORB_DEV + STO_DEV, NG, NG, NG)
    results = lax.map(lambda group: chebyshev(group, field_slab, kinetic, cheb_coefs), groups)
    results = results.reshape(ORBITALS + STOCHASTIC, NG, NYZ)
    density = lax.optimization_barrier(jnp.sum(results * results, axis=0)) / float(ORBITALS + STOCHASTIC)
    noise_out = results[ORBITALS:]
    return (density, margins, noise_out)
```

```python
import math

import jax
import jax.numpy as jnp
import ml_dtypes
import numpy as np
from jax import lax
from jax.experimental import pallas as pl
from jax.experimental.pallas import tpu as pltpu
from jax.sharding import PartitionSpec as P

NG = 96
ORDER = 6
ROWS = 72
XS = 104
UX, UY, UR = 24, 6, 8
MESH = pl.DeviceIdType.MESH
ORB_OWNER = tuple(8 * i + 2 * (1 - i % 2) for i in range(4))
STO_OWNER = tuple(4 * s + 2 * ((s // 2) % 2) for s in range(8))


def tables():
    index = np.arange(NG)
    phase = 2.0 * np.pi / NG * ((index[:, None] * index[None, :]) % NG)
    hartley = (np.cos(phase) + np.sin(phase)) / math.sqrt(NG)
    wave = np.minimum(index, NG - index) / (NG / 2.0)
    doubled = 2.0 * (hartley @ (((wave * wave - 0.5) / 3.0)[:, None] * hartley))
    high = doubled.astype(ml_dtypes.bfloat16)
    low = (doubled - high.astype(np.float64)).astype(ml_dtypes.bfloat16)

    def left(order):
        h, l = high[order][:, order], low[order][:, order]
        return np.block([[h, h], [l, l]])

    right = np.zeros((256, 256), ml_dtypes.bfloat16)
    for at in (0, 128):
        right[at : at + NG, 0:NG] = high
        right[at : at + NG, 128 : 128 + NG] = low
    y_order = np.array([4 * (q % 24) + q // 24 for q in range(NG)])
    return left(index), left(y_order), right


def halves(t):
    high = t.astype(jnp.bfloat16)
    return high, (t - high.astype(jnp.float32)).astype(jnp.bfloat16)


def left_mul(matrix, a, b):
    right = jnp.concatenate(
        [jnp.concatenate([a[0], b[0]], 1), jnp.concatenate([a[1], b[1]], 1)], 0
    )
    out = jnp.dot(matrix, right, preferred_element_type=jnp.float32)
    out = out[:NG] + out[NG:]
    return out[:, :128], out[:, 128:]


def spread(a, lane):
    zero = jnp.zeros((24, 128), jnp.float32)
    one = jnp.where(lane < 32, pltpu.roll(a[0], 32, 1), pltpu.roll(a[1], 32, 1))
    two = jnp.where(lane < 64, pltpu.roll(a[1], 64, 1), pltpu.roll(a[2], 64, 1))
    parts = (a[0], one, two, pltpu.roll(a[2], 96, 1))
    return [jnp.where(lane < 96, part, zero) for part in parts]


def pack(b, lane):
    one = pltpu.roll(b[1], 96, 1)
    two = pltpu.roll(b[2], 64, 1)
    return (
        jnp.where(lane < 96, b[0], one),
        jnp.where(lane < 64, one, two),
        jnp.where(lane < 32, two, pltpu.roll(b[3], 32, 1)),
    )


def quarter(x, j):
    return pl.ds(pl.multiple_of(x * XS + 24 * j, 8), 24)


def filter_vector(land, pot_ref, kx_ref, ky_ref, wz_ref, coef_ref, T, W, FI, PO):
    lane = lax.broadcasted_iota(jnp.int32, (24, 128), 1)
    first_coef = coef_ref[0]

    @pl.loop(0, NG, step=UR)
    def _(base):
        for u in range(UR):
            x = base + u
            for j, part in enumerate(spread([land[x, pl.ds(k, 24, stride=3), :] for k in range(3)], lane)):
                T[0, quarter(x, j), :] = part
                FI[quarter(x, j), :] = first_coef * part
            for j, part in enumerate(spread([pot_ref[x, pl.ds(k, 24, stride=3), :] for k in range(3)], lane)):
                PO[quarter(x, j), :] = 2.0 * part

    @pl.loop(0, ORDER)
    def _(k):
        now = lax.rem(k, 2)
        other = 1 - now
        alpha = jnp.where(k == 0, 0.5, 1.0)
        beta = jnp.where(k == 0, 0.0, 1.0)
        coef = coef_ref[k + 1]

        @pl.loop(0, NG, step=2 * UX)
        def _(base):
            for u in range(UX):
                y = base + 2 * u
                columns = [pl.ds(y + q, NG, stride=XS) for q in range(2)]
                outs = left_mul(kx_ref[...], *[halves(T[now, c, :]) for c in columns])
                for c, out in zip(columns, outs):
                    W[c, :] = out

        @pl.loop(0, NG, step=2 * UY)
        def _(base):
            rows = [pl.ds(pl.multiple_of((base + q) * XS, 8), NG) for q in range(2 * UY)]
            held = [T[now, r, :] for r in rows]
            split = [halves(t) for t in held]
            along_y = []
            for u in range(UY):
                along_y += left_mul(ky_ref[...], split[2 * u], split[2 * u + 1])
            stacked = jnp.concatenate([jnp.concatenate(pair, 1) for pair in split], 0)
            along_z = jnp.dot(stacked, wz_ref[...], preferred_element_type=jnp.float32)
            for q, r in enumerate(rows):
                z = along_z[NG * q : NG * (q + 1)]
                total = z[:, :128] + z[:, 128:] + along_y[q] + W[r, :] + PO[r, :] * held[q]
                following = alpha * total - beta * T[other, r, :]
                T[other, r, :] = following
                FI[r, :] = FI[r, :] + coef * following

    @pl.loop(0, NG, step=UR)
    def _(base):
        for u in range(UR):
            x = base + u
            for k, part in enumerate(pack([FI[quarter(x, j), :] for j in range(4)], lane)):
                land[x, pl.ds(k, 24, stride=3), :] = part


def filter_kernel(
    orb_ref, sto_ref, pot_ref, kx_ref, ky_ref, wz_ref, coef_ref, orb_out, sto_out,
    land, T, W, FI, PO, send_sems, land_sem, orb_sem, sto_sem, out_sem,
):
    me = lax.axis_index("grid")
    level = me // 4
    planes = land.at[pl.ds(3 * me, 3)]
    sources = [(orb_ref.at[:, :, i, :], t) for i, t in enumerate(ORB_OWNER)]
    sources += [(sto_ref.at[:, :, s, :], t) for s, t in enumerate(STO_OWNER)]

    def to_owner(v):
        return pltpu.make_async_remote_copy(
            src_ref=sources[v][0], dst_ref=planes, send_sem=send_sems.at[v], recv_sem=land_sem,
            device_id={"grid": sources[v][1]}, device_id_type=MESH,
        )

    for v in range(12):
        @pl.when(me != sources[v][1])
        def _():
            to_owner(v).start()

        @pl.when(me == sources[v][1])
        def _():
            pltpu.make_async_copy(sources[v][0], planes, land_sem).start()

    turned = (level // 2) % 2
    row = (me // 2) % 2
    first_core = me % 2 == 0
    is_sto = jnp.logical_and(first_core, row == turned)
    is_orb = jnp.logical_and(first_core, jnp.logical_and(row != turned, level % 2 == 0))

    @pl.when(jnp.logical_or(is_sto, is_orb))
    def _():
        pltpu.make_async_copy(land, land, land_sem).wait()
        filter_vector(land, pot_ref, kx_ref, ky_ref, wz_ref, coef_ref, T, W, FI, PO)

    def hand_back(out, at, sem):
        @pl.loop(0, 32)
        def _(d):
            src = land.at[pl.ds(3 * d, 3)]

            @pl.when(d != me)
            def _():
                pltpu.make_async_remote_copy(
                    src_ref=src, dst_ref=out.at[:, :, at, :], send_sem=out_sem, recv_sem=sem,
                    device_id={"grid": d}, device_id_type=MESH,
                ).start()

            @pl.when(d == me)
            def _():
                pltpu.make_async_copy(src, out.at[:, :, at, :], sem).start()

        sent = land.at[pl.ds(0, 93)]
        pltpu.make_async_copy(sent, sent, out_sem).wait()

    for i in range(4):
        @pl.when(me == ORB_OWNER[i])
        def _():
            hand_back(orb_out, i, orb_sem)

    for s in range(8):
        @pl.when(me == STO_OWNER[s])
        def _():
            hand_back(sto_out, s, sto_sem)

    pltpu.make_async_copy(orb_out, orb_out, orb_sem).wait()
    pltpu.make_async_copy(sto_out, sto_out, sto_sem).wait()
    for v in range(12):
        @pl.when(me != sources[v][1])
        def _():
            to_owner(v).wait_send()


def filter_all(orbitals, noise, potential, coefs):
    vmem = pl.BlockSpec(memory_space=pltpu.VMEM)
    anywhere = pl.BlockSpec(memory_space=pl.ANY)
    f32 = jnp.float32
    field = pltpu.VMEM((NG * XS, 128), f32)
    return pl.pallas_call(
        filter_kernel,
        out_shape=(
            jax.ShapeDtypeStruct((3, ROWS, 4, 128), f32),
            jax.ShapeDtypeStruct((3, ROWS, 8, 128), f32),
        ),
        in_specs=[anywhere, anywhere] + [vmem] * 4 + [pl.BlockSpec(memory_space=pltpu.SMEM)],
        out_specs=(anywhere, anywhere),
        scratch_shapes=[
            pltpu.VMEM((NG, ROWS, 128), f32),
            pltpu.VMEM((2, NG * XS, 128), f32),
            field, field, field,
            pltpu.SemaphoreType.DMA((12,)),
            pltpu.SemaphoreType.DMA, pltpu.SemaphoreType.DMA,
            pltpu.SemaphoreType.DMA, pltpu.SemaphoreType.DMA,
        ],
        compiler_params=pltpu.CompilerParams(
            vmem_limit_bytes=56 * 2**20, has_side_effects=True
        ),
    )(orbitals, noise, potential, *[jnp.asarray(t) for t in tables()], coefs)


def to_rows(block):
    vectors = block.shape[0]
    return block.reshape(vectors, 3, ROWS, 128).transpose(1, 2, 0, 3)


def from_rows(block):
    vectors = block.shape[2]
    return block.transpose(2, 0, 1, 3).reshape(vectors, 3, ROWS * 128)


def local(orbitals, sign_vectors, potential, cheb_coefs):
    high = lax.Precision.HIGHEST
    scale_root = math.sqrt(float(NG) ** 3)
    noise = sign_vectors.astype(jnp.float32)
    whole_potential = lax.all_gather(potential, "grid", axis=0, tiled=True)
    gathered = lax.all_gather(orbitals, "band", axis=0, tiled=True)
    partial_margin = jnp.einsum("ipn,spn->is", gathered, noise, precision=high)
    margins = lax.psum(partial_margin, "grid") / scale_root
    correction = jnp.einsum("is,ipn->spn", margins, gathered, precision=high)
    projected = noise - correction / scale_root
    orb_rows, sto_rows = filter_all(
        to_rows(orbitals), to_rows(projected), whole_potential.reshape(NG, ROWS, 128), cheb_coefs
    )
    squares = (jnp.sum(orb_rows * orb_rows, axis=2) + jnp.sum(sto_rows * sto_rows, axis=2)) / 96.0
    squares = squares.reshape(3, NG * NG)
    density = lax.psum_scatter(squares, "band", scatter_dimension=1, tiled=True)
    return (density, margins, from_rows(sto_rows))


def solution(mesh):
    return jax.shard_map(
        local,
        mesh=mesh,
        in_specs=(P("band", "grid", None), P("band", "grid", None), P("grid", None), P()),
        out_specs=(P("grid", "band"), P(None, "band"), P("band", "grid", None)),
        check_vma=False,
    )
```

```python
import math

import jax
import jax.numpy as jnp
import ml_dtypes
import numpy as np
from jax import lax
from jax.experimental import pallas as pl
from jax.experimental.pallas import tpu as pltpu
from jax.sharding import PartitionSpec as P

NG = 96
ORDER = 6
ROWS = 72
XS = 104
UX, UY, UR = 24, 6, 8
BANDS = 8
CHUNK = ROWS // BANDS
SCALE = math.sqrt(float(NG) ** 3)
MESH = pl.DeviceIdType.MESH
ORB_OWNER = tuple(8 * i + 2 * (1 - i % 2) for i in range(4))
STO_OWNER = tuple(4 * s + 2 * ((s // 2) % 2) for s in range(8))


def tables():
    index = np.arange(NG)
    phase = 2.0 * np.pi / NG * ((index[:, None] * index[None, :]) % NG)
    hartley = (np.cos(phase) + np.sin(phase)) / math.sqrt(NG)
    wave = np.minimum(index, NG - index) / (NG / 2.0)
    doubled = 2.0 * (hartley @ (((wave * wave - 0.5) / 3.0)[:, None] * hartley))
    high = doubled.astype(ml_dtypes.bfloat16)
    low = (doubled - high.astype(np.float64)).astype(ml_dtypes.bfloat16)

    def left(order):
        h, l = high[order][:, order], low[order][:, order]
        return np.block([[h, h], [l, l]])

    right = np.zeros((256, 256), ml_dtypes.bfloat16)
    for at in (0, 128):
        right[at : at + NG, 0:NG] = high
        right[at : at + NG, 128 : 128 + NG] = low
    y_order = np.array([4 * (q % 24) + q // 24 for q in range(NG)])
    return left(index), left(y_order), right


def halves(t):
    high = t.astype(jnp.bfloat16)
    return high, (t - high.astype(jnp.float32)).astype(jnp.bfloat16)


def left_mul(matrix, a, b):
    right = jnp.concatenate(
        [jnp.concatenate([a[0], b[0]], 1), jnp.concatenate([a[1], b[1]], 1)], 0
    )
    out = jnp.dot(matrix, right, preferred_element_type=jnp.float32)
    out = out[:NG] + out[NG:]
    return out[:, :128], out[:, 128:]


def spread(a, lane):
    zero = jnp.zeros(lane.shape, jnp.float32)
    one = jnp.where(lane < 32, pltpu.roll(a[0], 32, 1), pltpu.roll(a[1], 32, 1))
    two = jnp.where(lane < 64, pltpu.roll(a[1], 64, 1), pltpu.roll(a[2], 64, 1))
    parts = (a[0], one, two, pltpu.roll(a[2], 96, 1))
    return [jnp.where(lane < 96, part, zero) for part in parts]


def pack(b, lane):
    one = pltpu.roll(b[1], 96, 1)
    two = pltpu.roll(b[2], 64, 1)
    return (
        jnp.where(lane < 96, b[0], one),
        jnp.where(lane < 64, one, two),
        jnp.where(lane < 32, two, pltpu.roll(b[3], 32, 1)),
    )


def quarter(x, j):
    return pl.ds(pl.multiple_of(x * XS + 24 * j, 8), 24)


def wait(view, sem):
    pltpu.make_async_copy(view, view, sem).wait()


def remote(src, dst, send, recv, device):
    return pltpu.make_async_remote_copy(
        src_ref=src, dst_ref=dst, send_sem=send, recv_sem=recv, device_id=device, device_id_type=MESH
    )


def concat_rows(ref, p, kind):
    return jnp.concatenate([ref[p, r].astype(jnp.float32).astype(kind) for r in range(CHUNK)], 1)


def against(a, b, contract):
    return lax.dot_general(a, b, (((1,), (contract,)), ((), ())), preferred_element_type=jnp.float32)


def everything(
    orb, sto, potc, kx, ky, wz, coef_ref, sto_out, mar_out, den_out,
    land, landi, T, W, FI, PO, pot1, pot2, a_orb, a_sto, mt, rs, own_sum, gs, own_mar, ms,
    orb_home, a_f, cbuf, c_home, sto_home, sq, sq_in,
    in_sems, pot1_send, pot1_recv, pot2_send, pot2_recv, land_sem, landi_sem,
    ao_send, ao_recv, as_send, as_recv, rs_send, rs_recv, gs_send, gs_recv, ms_send, ms_recv,
    out_send, oh_recv, sh_recv, af_send, af_recv, c_send, c_recv, sq_send, sq_recv,
):
    me = lax.axis_index("grid")
    band = lax.axis_index("band")
    level = me // 4
    seat = me % 4
    f32 = jnp.float32

    barrier = pltpu.get_barrier_semaphore()
    for j in range(1, 32):
        pl.semaphore_signal(barrier, inc=1, device_id={"grid": lax.rem(me + j, 32)}, device_id_type=MESH)
        other = lax.rem(band * 4 + seat + j, 32)
        pl.semaphore_signal(
            barrier, inc=1, device_id={"band": other // 4, "grid": level * 4 + other % 4}, device_id_type=MESH
        )
    pl.semaphore_wait(barrier, 62)

    turned = (level // 2) % 2
    row = seat // 2
    first_core = seat % 2 == 0
    is_sto = jnp.logical_and(first_core, row == turned)
    is_orb = jnp.logical_and(first_core, jnp.logical_and(row != turned, level % 2 == 0))
    is_owner = jnp.logical_or(is_sto, is_orb)

    def share(d):
        return remote(
            potc, pot1.at[pl.ds(pl.multiple_of(32 * level, 32), 32)], pot1_send, pot1_recv,
            {"grid": lax.rem(level + d, 8) * 4 + seat},
        )

    pltpu.make_async_copy(potc, pot1.at[pl.ds(pl.multiple_of(32 * level, 32), 32)], pot1_recv).start()
    for d in range(1, 8):
        share(d).start()

    def to_owner(v):
        if v < 4:
            return remote(
                orb.at[:, :, v, :], land.at[pl.ds(3 * me, 3)], in_sems.at[v], land_sem, {"grid": ORB_OWNER[v]}
            )
        return remote(
            sto.at[:, :, v - 4, :], landi.at[pl.ds(3 * me, 3)], in_sems.at[v], landi_sem, {"grid": STO_OWNER[v - 4]}
        )

    def send_vectors(low, high):
        for v in range(low, high):
            target = (ORB_OWNER + STO_OWNER)[v]

            @pl.when(me != target)
            def _():
                to_owner(v).start()

            @pl.when(me == target)
            def _():
                if v < 4:
                    pltpu.make_async_copy(orb.at[:, :, v, :], land.at[pl.ds(3 * me, 3)], land_sem).start()
                else:
                    pltpu.make_async_copy(sto.at[:, :, v - 4, :], landi.at[pl.ds(3 * me, 3)], landi_sem).start()

    send_vectors(0, 4)

    wait(pot1, pot1_recv)
    place = pot2.at[pl.ds(pl.multiple_of(256 * (band * 4 + seat), 256), 256)]

    def to_level(kind, d):
        seat_to = 2 * turned if kind == 0 else 2 * (1 - turned)
        return remote(
            pot1, place, pot2_send.at[8 * kind + d], pot2_recv,
            {"band": lax.rem(band + d, BANDS), "grid": level * 4 + seat_to},
        )

    def goes(kind, d):
        go = seat != (2 * turned if kind == 0 else 2 * (1 - turned)) if d == 0 else seat >= 0
        return jnp.logical_and(go, level % 2 == 0) if kind == 1 else go

    for d in range(8):
        for kind in range(2):
            @pl.when(goes(kind, d))
            def _():
                to_level(kind, d).start()

    @pl.when(is_owner)
    def _():
        pltpu.make_async_copy(pot1, place, pot2_recv).start()

    send_vectors(4, 12)

    def cells(src, dst, count, to, sends, recvs):
        return remote(
            src.at[:, pl.ds(CHUNK * to, CHUNK)], dst.at[:, :, pl.ds(pl.multiple_of(count * band, count), count), :],
            sends, recvs, {"band": to},
        )

    def own_cells(src, dst, count, recvs):
        pltpu.make_async_copy(
            src.at[:, pl.ds(CHUNK * band, CHUNK)],
            dst.at[:, :, pl.ds(pl.multiple_of(count * band, count), count), :], recvs,
        ).start()

    own_cells(orb, a_orb, 4, ao_recv)
    own_cells(sto, a_sto, 8, as_recv)
    for d in range(1, 8):
        to = lax.rem(band + d, BANDS)
        cells(orb, a_orb, 4, to, ao_send, ao_recv).start()
        cells(sto, a_sto, 8, to, as_send, as_recv).start()

    def eight(ref, at):
        return ref.at[pl.ds(pl.multiple_of(8 * at, 8), 8)]

    def service_partial():
        wait(a_orb, ao_recv)
        wait(a_sto, as_recv)
        total = jnp.zeros((64, 32), f32)
        for p in range(3):
            signs = concat_rows(a_sto, p, jnp.bfloat16)
            for part in halves(concat_rows(a_orb, p, f32)):
                total += against(signs, part, 1)
        mt[...] = jnp.zeros((64, 128), f32)
        mt[:, 0:32] = total
        pltpu.make_async_copy(eight(mt, band), eight(rs, band), rs_recv).start()
        for d in range(1, 8):
            to = lax.rem(band + d, BANDS)
            remote(eight(mt, to), eight(rs, band), rs_send, rs_recv, {"band": to}).start()

    def service_slab():
        wait(rs, rs_recv)
        own_sum[...] = sum(rs[8 * j : 8 * j + 8, :] for j in range(8))
        pltpu.make_async_copy(own_sum, eight(gs, me), gs_recv).start()

        @pl.loop(1, 32)
        def _(d):
            remote(own_sum, eight(gs, me), gs_send, gs_recv, {"grid": lax.rem(me + d, 32)}).start()

    def service_whole():
        wait(gs, gs_recv)
        margins = sum(gs[8 * j : 8 * j + 8, :] for j in range(32)) / SCALE
        own_mar[...] = margins
        mar_out[...] = margins
        pltpu.make_async_copy(own_mar, eight(ms, band), ms_recv).start()
        for d in range(1, 8):
            remote(own_mar, eight(ms, band), ms_send, ms_recv, {"band": lax.rem(band + d, BANDS)}).start()

    services = (service_partial, service_slab, service_whole)

    @pl.when(jnp.logical_not(is_owner))
    def _():
        for service in services:
            service()

    @pl.when(is_owner)
    def _():
        small = lax.broadcasted_iota(jnp.int32, (8, 128), 1)
        wait(pot2, pot2_recv)

        @pl.loop(0, 32)
        def _(q):
            for p in range(3):
                for m in range(3):
                    parts = spread([pot2[pl.ds(q * 256 + p * 9 + 3 * m + k, 8, stride=32), :] for k in range(3)], small)
                    for j, part in enumerate(parts):
                        at = (3 * (q % 4) + p) * XS + 24 * j + 3 * (q // 4) + m
                        PO[pl.ds(at, 8, stride=12 * XS), :] = 2.0 * part

        lane = lax.broadcasted_iota(jnp.int32, (24, 128), 1)
        first_coef = coef_ref[0]

        def take(source):
            @pl.loop(0, NG, step=UR)
            def _(base):
                for u in range(UR):
                    x = base + u
                    rows = [source[x, pl.ds(k, 24, stride=3), :].astype(f32) for k in range(3)]
                    for j, part in enumerate(spread(rows, lane)):
                        T[0, quarter(x, j), :] = part
                        FI[quarter(x, j), :] = first_coef * part

        @pl.when(is_orb)
        def _():
            wait(land, land_sem)
            take(land)

        @pl.when(is_sto)
        def _():
            wait(landi, landi_sem)
            take(landi)

        @pl.loop(0, ORDER)
        def _(k):
            for at, service in enumerate(services):
                @pl.when(k == 2 + at)
                def _():
                    service()

            apply_operator(k, kx, ky, wz, coef_ref, T, W, FI, PO)

        @pl.loop(0, NG, step=UR)
        def _(base):
            for u in range(UR):
                x = base + u
                for k, part in enumerate(pack([FI[quarter(x, j), :] for j in range(4)], lane)):
                    land[x, pl.ds(k, 24, stride=3), :] = part

    def hand_back(home, at, recv):
        pltpu.make_async_copy(land.at[pl.ds(3 * me, 3)], home.at[:, :, at, :], recv).start()

        @pl.loop(1, 32)
        def _(d):
            to = lax.rem(me + d, 32)
            remote(land.at[pl.ds(3 * to, 3)], home.at[:, :, at, :], out_send, recv, {"grid": to}).start()

    for v, target in enumerate(ORB_OWNER + STO_OWNER):
        @pl.when(me == target)
        def _():
            hand_back(*((orb_home, v, oh_recv) if v < 4 else (sto_home, v - 4, sh_recv)))

    wait(orb_home, oh_recv)
    own_cells(orb_home, a_f, 4, af_recv)
    for d in range(1, 8):
        cells(orb_home, a_f, 4, lax.rem(band + d, BANDS), af_send, af_recv).start()
    wait(ms, ms_recv)
    m_high, m_low = halves(ms[:, 0:32] * (1.0 / SCALE))
    wait(a_f, af_recv)
    orb_squares = []
    for p in range(3):
        field = concat_rows(a_f, p, f32)
        f_high, f_low = halves(field)
        change = against(m_high, f_high, 0) + against(m_high, f_low, 0) + against(m_low, f_high, 0)
        summed = jnp.sum(field * field, axis=0, keepdims=True)
        for r in range(CHUNK):
            cbuf[p, r] = change[:, 128 * r : 128 * r + 128]
            orb_squares.append(summed[:, 128 * r : 128 * r + 128])

    def back(to):
        return remote(
            cbuf.at[:, :, pl.ds(pl.multiple_of(8 * to, 8), 8), :], c_home.at[:, pl.ds(CHUNK * band, CHUNK)],
            c_send, c_recv, {"band": to},
        )

    pltpu.make_async_copy(
        cbuf.at[:, :, pl.ds(pl.multiple_of(8 * band, 8), 8), :], c_home.at[:, pl.ds(CHUNK * band, CHUNK)], c_recv
    ).start()
    for d in range(1, 8):
        back(lax.rem(band + d, BANDS)).start()

    wait(c_home, c_recv)
    wait(sto_home, sh_recv)

    @pl.loop(0, BANDS)
    def _(b):
        for p in range(3):
            for r in range(CHUNK):
                at = b * CHUNK + r
                value = sto_home[p, at] - c_home[p, at]
                sto_out[p, at] = value
                sq[b, pl.ds(p * CHUNK + r, 1), :] = jnp.sum(value * value, axis=0, keepdims=True)

    pltpu.make_async_copy(sq.at[band], sq_in.at[band], sq_recv).start()
    for d in range(1, 8):
        to = lax.rem(band + d, BANDS)
        remote(sq.at[to], sq_in.at[band], sq_send, sq_recv, {"band": to}).start()
    wait(sq_in, sq_recv)
    for at, orbital_part in enumerate(orb_squares):
        den_out[at : at + 1, :] = orbital_part
    den_out[...] = (den_out[...] + sum(sq_in[b] for b in range(BANDS))) / 96.0

    wait(pot1.at[pl.ds(0, 224)], pot1_send)
    for d in range(8):
        for kind in range(2):
            @pl.when(goes(kind, d))
            def _():
                to_level(kind, d).wait_send()
    for v, target in enumerate(ORB_OWNER + STO_OWNER):
        @pl.when(me != target)
        def _():
            to_owner(v).wait_send()
    wait(orb.at[:, pl.ds(0, 7 * CHUNK)], ao_send)
    wait(sto.at[:, pl.ds(0, 7 * CHUNK)], as_send)
    wait(rs.at[pl.ds(0, 56)], rs_send)
    wait(gs.at[pl.ds(0, 248)], gs_send)
    wait(ms.at[pl.ds(0, 56)], ms_send)

    @pl.when(is_owner)
    def _():
        wait(land.at[pl.ds(0, 93)], out_send)

    wait(orb_home.at[:, pl.ds(0, 7 * CHUNK)], af_send)
    wait(c_home.at[:, pl.ds(0, 7 * CHUNK)], c_send)
    wait(sq.at[pl.ds(0, 7)], sq_send)


def apply_operator(k, kx_ref, ky_ref, wz_ref, coef_ref, T, W, FI, PO):
    now = lax.rem(k, 2)
    other = 1 - now
    alpha = jnp.where(k == 0, 0.5, 1.0)
    beta = jnp.where(k == 0, 0.0, 1.0)
    coef = coef_ref[k + 1]

    @pl.loop(0, NG, step=2 * UX)
    def _(base):
        for u in range(UX):
            y = base + 2 * u
            columns = [pl.ds(y + q, NG, stride=XS) for q in range(2)]
            outs = left_mul(kx_ref[...], *[halves(T[now, c, :]) for c in columns])
            for c, out in zip(columns, outs):
                W[c, :] = out

    @pl.loop(0, NG, step=2 * UY)
    def _(base):
        rows = [pl.ds(pl.multiple_of((base + q) * XS, 8), NG) for q in range(2 * UY)]
        held = [T[now, r, :] for r in rows]
        split = [halves(t) for t in held]
        along_y = []
        for u in range(UY):
            along_y += left_mul(ky_ref[...], split[2 * u], split[2 * u + 1])
        stacked = jnp.concatenate([jnp.concatenate(pair, 1) for pair in split], 0)
        along_z = jnp.dot(stacked, wz_ref[...], preferred_element_type=jnp.float32)
        for q, r in enumerate(rows):
            z = along_z[NG * q : NG * (q + 1)]
            total = z[:, :128] + z[:, 128:] + along_y[q] + W[r, :] + PO[r, :] * held[q]
            following = alpha * total - beta * T[other, r, :]
            T[other, r, :] = following
            FI[r, :] = FI[r, :] + coef * following


def to_rows(block):
    vectors = block.shape[0]
    return block.reshape(vectors, 3, ROWS, 128).transpose(1, 2, 0, 3)


def from_rows(block):
    vectors = block.shape[2]
    return block.transpose(2, 0, 1, 3).reshape(vectors, 3, ROWS * 128)


def local(orbitals, sign_vectors, potential, cheb_coefs):
    f32 = jnp.float32
    vmem = pl.BlockSpec(memory_space=pltpu.VMEM)
    anywhere = pl.BlockSpec(memory_space=pl.ANY)
    share = lax.dynamic_slice_in_dim(potential, lax.axis_index("band") * (CHUNK * 128), CHUNK * 128, 1)
    share = jnp.pad(share.reshape(3 * CHUNK, 128), ((0, 5), (0, 0)))
    field = pltpu.VMEM((NG * XS, 128), f32)
    dma = pltpu.SemaphoreType.DMA
    noise, margins, density = pl.pallas_call(
        everything,
        out_shape=(
            jax.ShapeDtypeStruct((3, ROWS, 8, 128), f32),
            jax.ShapeDtypeStruct((8, 128), f32),
            jax.ShapeDtypeStruct((3 * CHUNK, 128), f32),
        ),
        in_specs=[anywhere, anywhere] + [vmem] * 4 + [pl.BlockSpec(memory_space=pltpu.SMEM)],
        out_specs=(vmem, vmem, vmem),
        scratch_shapes=[
            pltpu.VMEM((NG, ROWS, 128), f32),
            pltpu.VMEM((NG, ROWS, 128), jnp.int32),
            pltpu.VMEM((2, NG * XS, 128), f32),
            field, field, field,
            pltpu.VMEM((256, 128), f32),
            pltpu.VMEM((8192, 128), f32),
            pltpu.VMEM((3, CHUNK, 32, 128), f32),
            pltpu.VMEM((3, CHUNK, 64, 128), jnp.int32),
            pltpu.VMEM((64, 128), f32),
            pltpu.VMEM((64, 128), f32),
            pltpu.VMEM((8, 128), f32),
            pltpu.VMEM((256, 128), f32),
            pltpu.VMEM((8, 128), f32),
            pltpu.VMEM((64, 128), f32),
            pltpu.VMEM((3, ROWS, 4, 128), f32),
            pltpu.VMEM((3, CHUNK, 32, 128), f32),
            pltpu.VMEM((3, CHUNK, 64, 128), f32),
            pltpu.VMEM((3, ROWS, 8, 128), f32),
            pltpu.VMEM((3, ROWS, 8, 128), f32),
            pltpu.VMEM((BANDS, 3 * CHUNK, 128), f32),
            pltpu.VMEM((BANDS, 3 * CHUNK, 128), f32),
            dma((12,)), dma, dma, dma((16,)), dma, dma, dma,
            dma, dma, dma, dma, dma, dma, dma, dma, dma, dma,
            dma, dma, dma, dma, dma, dma, dma, dma, dma,
        ],
        compiler_params=pltpu.CompilerParams(
            vmem_limit_bytes=60 * 2**20, has_side_effects=True, collective_id=1
        ),
    )(
        to_rows(orbitals), to_rows(sign_vectors), share,
        *[jnp.asarray(t) for t in tables()], cheb_coefs,
    )
    return density.reshape(3, CHUNK * 128), margins[:, :32].T, from_rows(noise)


def solution(mesh):
    return jax.shard_map(
        local,
        mesh=mesh,
        in_specs=(P("band", "grid", None), P("band", "grid", None), P("grid", None), P()),
        out_specs=(P("grid", "band"), P(None, "band"), P("band", "grid", None)),
        check_vma=False,
    )
```

```python
import math

import jax
import jax.numpy as jnp
import ml_dtypes
import numpy as np
from jax import lax
from jax.experimental import pallas as pl
from jax.experimental.pallas import tpu as pltpu
from jax.sharding import PartitionSpec as P

NG = 96
ORDER = 6
ROWS = 72
XS = 104
UX, UY, UR = 24, 12, 8
SHARE = 56
BLOCK = 16 * SHARE
BANDS = 8
CHUNK = ROWS // BANDS
SCALE = math.sqrt(float(NG) ** 3)
MESH = pl.DeviceIdType.MESH
ORB_OWNER = tuple(8 * i + 2 * (1 - i % 2) for i in range(4))
STO_OWNER = tuple(4 * s + 2 * ((s // 2) % 2) for s in range(8))


def tables():
    index = np.arange(NG)
    phase = 2.0 * np.pi / NG * ((index[:, None] * index[None, :]) % NG)
    hartley = (np.cos(phase) + np.sin(phase)) / math.sqrt(NG)
    wave = np.minimum(index, NG - index) / (NG / 2.0)
    doubled = 2.0 * (hartley @ (((wave * wave - 0.5) / 3.0)[:, None] * hartley))
    high = doubled.astype(ml_dtypes.bfloat16)
    low = (doubled - high.astype(np.float64)).astype(ml_dtypes.bfloat16)

    def left(order):
        h, l = high[order][:, order], low[order][:, order]
        return np.block([[h, h], [l, l]])

    right = np.zeros((256, 256), ml_dtypes.bfloat16)
    for at in (0, 128):
        right[at : at + NG, 0:NG] = high
        right[at : at + NG, 128 : 128 + NG] = low
    y_order = np.array([4 * (q % 24) + q // 24 for q in range(NG)])
    return left(index), left(y_order), right


def halves(t):
    high = t.astype(jnp.bfloat16)
    return high, (t - high.astype(jnp.float32)).astype(jnp.bfloat16)


def left_mul(matrix, a, b):
    right = jnp.concatenate(
        [jnp.concatenate([a[0], b[0]], 1), jnp.concatenate([a[1], b[1]], 1)], 0
    )
    out = jnp.dot(matrix, right, preferred_element_type=jnp.float32)
    out = out[:NG] + out[NG:]
    return out[:, :128], out[:, 128:]


def spread(a, lane):
    zero = jnp.zeros(lane.shape, jnp.float32)
    one = jnp.where(lane < 32, pltpu.roll(a[0], 32, 1), pltpu.roll(a[1], 32, 1))
    two = jnp.where(lane < 64, pltpu.roll(a[1], 64, 1), pltpu.roll(a[2], 64, 1))
    parts = (a[0], one, two, pltpu.roll(a[2], 96, 1))
    return [jnp.where(lane < 96, part, zero) for part in parts]


def pack(b, lane):
    one = pltpu.roll(b[1], 96, 1)
    two = pltpu.roll(b[2], 64, 1)
    return (
        jnp.where(lane < 96, b[0], one),
        jnp.where(lane < 64, one, two),
        jnp.where(lane < 32, two, pltpu.roll(b[3], 32, 1)),
    )


def quarter(x, j):
    return pl.ds(pl.multiple_of(x * XS + 24 * j, 8), 24)


def wait(view, sem):
    pltpu.make_async_copy(view, view, sem).wait()


def remote(src, dst, send, recv, device):
    return pltpu.make_async_remote_copy(
        src_ref=src, dst_ref=dst, send_sem=send, recv_sem=recv, device_id=device, device_id_type=MESH
    )


def concat_rows(ref, p, kind):
    return jnp.concatenate([ref[p, r].astype(jnp.float32).astype(kind) for r in range(CHUNK)], 1)


def against(a, b, contract):
    return lax.dot_general(a, b, (((1,), (contract,)), ((), ())), preferred_element_type=jnp.float32)


def everything(
    orb, sto, potc, kx, ky, wz, coef_ref, sto_out, mar_out, den_out,
    land, landi, T, W, FI, PO, pot2, a_orb, a_sto, mt, rs, own_sum, gs, own_mar, ms,
    orb_home, a_f, cbuf, c_home, sto_home, sq, sq_in,
    in_sems, pot1_send, pot1_recv, pot2_send, pot2_recv, pot3_send, pot3_recv, land_sem, landi_sem,
    ao_send, ao_recv, as_send, as_recv, rs_send, rs_recv, gs_send, gs_recv, ms_send, ms_recv,
    out_send, oh_recv, sh_recv, af_send, af_recv, c_send, c_recv, sq_send, sq_recv,
):
    me = lax.axis_index("grid")
    band = lax.axis_index("band")
    level = me // 4
    seat = me % 4
    f32 = jnp.float32

    barrier = pltpu.get_barrier_semaphore()
    for j in range(1, 32):
        pl.semaphore_signal(barrier, inc=1, device_id={"grid": lax.rem(me + j, 32)}, device_id_type=MESH)
    for j in range(1, BANDS):
        pl.semaphore_signal(barrier, inc=1, device_id={"band": lax.rem(band + j, BANDS)}, device_id_type=MESH)
    pl.semaphore_wait(barrier, 38)

    turned = (level // 2) % 2
    row = seat // 2
    core = seat % 2
    column = band % 4
    is_chip = jnp.logical_or(row == turned, level % 2 == 0)
    is_sto = jnp.logical_and(core == 0, row == turned)
    is_orb = jnp.logical_and(core == 0, jnp.logical_and(row != turned, level % 2 == 0))
    is_owner = jnp.logical_or(is_sto, is_orb)

    def block(a_core, a_column, blocks=1):
        return pot2.at[pl.ds(pl.multiple_of(BLOCK * (4 * a_core + a_column), 8), BLOCK * blocks)]

    slot = pot2.at[pl.ds(pl.multiple_of(BLOCK * (4 * core + column) + SHARE * (2 * level + row), 8), SHARE)]

    def share(kind, d):
        there = lax.rem(level + d, 8)
        row_to = (there // 2 + kind) % 2
        return remote(
            potc, slot, pot1_send.at[8 * kind + d], pot1_recv, {"grid": there * 4 + 2 * row_to + core}
        )

    def shares(kind, d):
        go = level >= 0 if kind == 0 else (level + d) % 2 == 0
        if d == 0:
            go = jnp.logical_and(go, row != turned if kind == 0 else row == turned)
        return go

    @pl.when(is_chip)
    def _():
        pltpu.make_async_copy(potc, slot, pot1_recv).start()

    for d in range(8):
        for kind in range(2):
            @pl.when(shares(kind, d))
            def _():
                share(kind, d).start()

    def to_owner(v):
        if v < 4:
            return remote(
                orb.at[:, :, v, :], land.at[pl.ds(3 * me, 3)], in_sems.at[v], land_sem, {"grid": ORB_OWNER[v]}
            )
        return remote(
            sto.at[:, :, v - 4, :], landi.at[pl.ds(3 * me, 3)], in_sems.at[v], landi_sem, {"grid": STO_OWNER[v - 4]}
        )

    def send_vectors(low, high):
        for v in range(low, high):
            target = (ORB_OWNER + STO_OWNER)[v]

            @pl.when(me != target)
            def _():
                to_owner(v).start()

            @pl.when(me == target)
            def _():
                if v < 4:
                    pltpu.make_async_copy(orb.at[:, :, v, :], land.at[pl.ds(3 * me, 3)], land_sem).start()
                else:
                    pltpu.make_async_copy(sto.at[:, :, v - 4, :], landi.at[pl.ds(3 * me, 3)], landi_sem).start()

    send_vectors(0, 4)

    def along(d):
        return remote(
            block(core, column), block(core, column), pot2_send, pot2_recv,
            {"band": (band // 4) * 4 + lax.rem(column + d, 4)},
        )

    @pl.when(is_chip)
    def _():
        wait(block(core, column), pot1_recv)
        for d in range(1, 4):
            along(d).start()

    send_vectors(4, 12)

    across = remote(
        block(1, 0, 4), block(1, 0, 4), pot3_send, pot3_recv, {"grid": level * 4 + 2 * row}
    )
    hands_over = jnp.logical_and(is_chip, core == 1)

    @pl.when(is_chip)
    def _():
        wait(block(0, 0, 3), pot2_recv)

        @pl.when(hands_over)
        def _():
            across.start()

    for v, target in enumerate(ORB_OWNER + STO_OWNER):
        @pl.when(me != target)
        def _():
            to_owner(v).wait_send()

    def cells(src, dst, count, to, sends, recvs):
        return remote(
            src.at[:, pl.ds(CHUNK * to, CHUNK)], dst.at[:, :, pl.ds(pl.multiple_of(count * band, count), count), :],
            sends, recvs, {"band": to},
        )

    def own_cells(src, dst, count, recvs):
        pltpu.make_async_copy(
            src.at[:, pl.ds(CHUNK * band, CHUNK)],
            dst.at[:, :, pl.ds(pl.multiple_of(count * band, count), count), :], recvs,
        ).start()

    own_cells(orb, a_orb, 4, ao_recv)
    own_cells(sto, a_sto, 8, as_recv)
    for d in range(1, 8):
        to = lax.rem(band + d, BANDS)
        cells(orb, a_orb, 4, to, ao_send, ao_recv).start()
        cells(sto, a_sto, 8, to, as_send, as_recv).start()

    def eight(ref, at):
        return ref.at[pl.ds(pl.multiple_of(8 * at, 8), 8)]

    def service_partial():
        wait(a_orb, ao_recv)
        wait(a_sto, as_recv)
        total = jnp.zeros((64, 32), f32)
        for p in range(3):
            signs = concat_rows(a_sto, p, jnp.bfloat16)
            for part in halves(concat_rows(a_orb, p, f32)):
                total += against(signs, part, 1)
        mt[...] = jnp.zeros((64, 128), f32)
        mt[:, 0:32] = total
        pltpu.make_async_copy(eight(mt, band), eight(rs, band), rs_recv).start()
        for d in range(1, 8):
            to = lax.rem(band + d, BANDS)
            remote(eight(mt, to), eight(rs, band), rs_send, rs_recv, {"band": to}).start()

    def service_slab():
        wait(rs, rs_recv)
        own_sum[...] = sum(rs[8 * j : 8 * j + 8, :] for j in range(8))
        pltpu.make_async_copy(own_sum, eight(gs, me), gs_recv).start()

        @pl.loop(1, 32)
        def _(d):
            remote(own_sum, eight(gs, me), gs_send, gs_recv, {"grid": lax.rem(me + d, 32)}).start()

    def service_whole():
        wait(gs, gs_recv)
        margins = sum(gs[8 * j : 8 * j + 8, :] for j in range(32)) / SCALE
        own_mar[...] = margins
        mar_out[...] = margins
        pltpu.make_async_copy(own_mar, eight(ms, band), ms_recv).start()
        for d in range(1, 8):
            remote(own_mar, eight(ms, band), ms_send, ms_recv, {"band": lax.rem(band + d, BANDS)}).start()

    services = (service_partial, service_slab, service_whole)

    @pl.when(jnp.logical_not(is_owner))
    def _():
        for service in services:
            service()

    @pl.when(is_owner)
    def _():
        wait(block(0, 0, 4), pot3_recv)
        small = lax.broadcasted_iota(jnp.int32, (16, 128), 1)

        @pl.loop(0, 8)
        def _(q):
            for p in range(3):
                for m in range(6):
                    parts = spread(
                        [pot2[pl.ds(q * BLOCK + p * 18 + 3 * m + k, 16, stride=SHARE), :] for k in range(3)], small
                    )
                    for j, part in enumerate(parts):
                        at = (3 * (q // 4) + p) * XS + 24 * j + 6 * (q % 4) + m
                        PO[pl.ds(at, 16, stride=6 * XS), :] = 2.0 * part

        lane = lax.broadcasted_iota(jnp.int32, (24, 128), 1)

        last_coef = coef_ref[ORDER]

        def take(source):
            @pl.loop(0, NG, step=UR)
            def _(base):
                for u in range(UR):
                    x = base + u
                    rows = [source[x, pl.ds(k, 24, stride=3), :].astype(f32) for k in range(3)]
                    for j, part in enumerate(spread(rows, lane)):
                        T[0, quarter(x, j), :] = last_coef * part
                        FI[quarter(x, j), :] = part

        @pl.when(is_orb)
        def _():
            wait(land, land_sem)
            take(land)

        @pl.when(is_sto)
        def _():
            wait(landi, landi_sem)
            take(landi)

        fields = (kx, ky, wz, coef_ref, T, W, FI, PO)
        apply_operator(0, 0, 1, UY, None, *fields)

        @pl.loop(1, ORDER - 1)
        def _(k):
            for at, service in enumerate(services[:2]):
                @pl.when(jnp.logical_and(is_sto, k == 3 + at))
                def _():
                    service()

            apply_operator(k, lax.rem(k, 2), 1 - lax.rem(k, 2), UY, None, *fields)

        def hand_back(base):
            for u in range(12):
                x = base + u
                for k, part in enumerate(pack([FI[quarter(x, j), :] for j in range(4)], lane)):
                    land[x, pl.ds(k, 24, stride=3), :] = part
            for u in range(4):
                to = base // 3 + u
                slab = land.at[pl.ds(3 * to, 3)]
                for kind, home, at, recv in (
                    (is_orb, orb_home, level // 2, oh_recv), (is_sto, sto_home, level, sh_recv)
                ):
                    @pl.when(jnp.logical_and(kind, to != me))
                    def _():
                        remote(slab, home.at[:, :, at, :], out_send, recv, {"grid": to}).start()

                    @pl.when(jnp.logical_and(kind, to == me))
                    def _():
                        pltpu.make_async_copy(slab, home.at[:, :, at, :], recv).start()

        apply_operator(ORDER - 1, 1, 0, 6, hand_back, *fields)

        @pl.when(is_orb)
        def _():
            service_partial()
            service_slab()

        service_whole()

    wait(orb_home, oh_recv)
    own_cells(orb_home, a_f, 4, af_recv)
    for d in range(1, 8):
        cells(orb_home, a_f, 4, lax.rem(band + d, BANDS), af_send, af_recv).start()
    wait(ms, ms_recv)
    m_high, m_low = halves(ms[:, 0:32] * (1.0 / SCALE))
    wait(a_f, af_recv)
    orb_squares = []
    for p in range(3):
        field = concat_rows(a_f, p, f32)
        f_high, f_low = halves(field)
        change = against(m_high, f_high, 0) + against(m_high, f_low, 0) + against(m_low, f_high, 0)
        summed = jnp.sum(field * field, axis=0, keepdims=True)
        for r in range(CHUNK):
            cbuf[p, r] = change[:, 128 * r : 128 * r + 128]
            orb_squares.append(summed[:, 128 * r : 128 * r + 128])

    def back(to):
        return remote(
            cbuf.at[:, :, pl.ds(pl.multiple_of(8 * to, 8), 8), :], c_home.at[:, pl.ds(CHUNK * band, CHUNK)],
            c_send, c_recv, {"band": to},
        )

    pltpu.make_async_copy(
        cbuf.at[:, :, pl.ds(pl.multiple_of(8 * band, 8), 8), :], c_home.at[:, pl.ds(CHUNK * band, CHUNK)], c_recv
    ).start()
    for d in range(1, 8):
        back(lax.rem(band + d, BANDS)).start()

    wait(c_home, c_recv)
    wait(sto_home, sh_recv)

    @pl.loop(0, BANDS)
    def _(b):
        for p in range(3):
            for r in range(CHUNK):
                at = b * CHUNK + r
                value = sto_home[p, at] - c_home[p, at]
                sto_out[p, at] = value
                sq[b, pl.ds(p * CHUNK + r, 1), :] = jnp.sum(value * value, axis=0, keepdims=True)

    pltpu.make_async_copy(sq.at[band], sq_in.at[band], sq_recv).start()
    for d in range(1, 8):
        to = lax.rem(band + d, BANDS)
        remote(sq.at[to], sq_in.at[band], sq_send, sq_recv, {"band": to}).start()
    wait(sq_in, sq_recv)
    noise_part = sum(sq_in[b] for b in range(BANDS))
    for p in range(3):
        for r in range(CHUNK):
            at = p * CHUNK + r
            den_out[p : p + 1, 128 * r : 128 * r + 128] = (orb_squares[at] + noise_part[at : at + 1]) / 96.0

    for d in range(8):
        for kind in range(2):
            @pl.when(shares(kind, d))
            def _():
                share(kind, d).wait_send()

    @pl.when(is_chip)
    def _():
        wait(block(0, 0, 3), pot2_send)

        @pl.when(hands_over)
        def _():
            across.wait_send()

    wait(orb.at[:, pl.ds(0, 7 * CHUNK)], ao_send)
    wait(sto.at[:, pl.ds(0, 7 * CHUNK)], as_send)
    wait(rs.at[pl.ds(0, 56)], rs_send)
    wait(gs.at[pl.ds(0, 248)], gs_send)
    wait(ms.at[pl.ds(0, 56)], ms_send)

    @pl.when(is_owner)
    def _():
        wait(land.at[pl.ds(0, 93)], out_send)

    wait(orb_home.at[:, pl.ds(0, 7 * CHUNK)], af_send)
    wait(c_home.at[:, pl.ds(0, 7 * CHUNK)], c_send)
    wait(sq.at[pl.ds(0, 7)], sq_send)


def apply_operator(k, now, other, group, emit, kx_ref, ky_ref, wz_ref, coef_ref, T, W, FI, PO):
    coef = coef_ref[ORDER - 1 - k]

    @pl.loop(0, NG, step=2 * UX)
    def _(base):
        for u in range(UX):
            y = base + 2 * u
            columns = [pl.ds(y + q, NG, stride=XS) for q in range(2)]
            outs = left_mul(kx_ref[...], *[halves(T[now, c, :]) for c in columns])
            for c, out in zip(columns, outs):
                W[c, :] = out

    @pl.loop(0, NG, step=2 * group)
    def _(base):
        rows = [pl.ds(pl.multiple_of((base + q) * XS, 8), NG) for q in range(2 * group)]
        held = [T[now, r, :] for r in rows]
        split = [halves(t) for t in held]
        for u in range(group):
            along_y = left_mul(ky_ref[...], split[2 * u], split[2 * u + 1])
            stacked = jnp.concatenate([jnp.concatenate(split[2 * u + q], 1) for q in range(2)], 0)
            along_z = jnp.dot(stacked, wz_ref[...], preferred_element_type=jnp.float32)
            for q in range(2):
                r = rows[2 * u + q]
                t = held[2 * u + q]
                z = along_z[NG * q : NG * (q + 1)]
                total = z[:, :128] + z[:, 128:] + along_y[q] + W[r, :] + PO[r, :] * t
                if emit is not None:
                    FI[r, :] = coef * FI[r, :] + 0.5 * total - T[other, r, :]
                elif isinstance(k, int):
                    T[other, r, :] = coef * FI[r, :] + total
                else:
                    T[other, r, :] = coef * FI[r, :] + total - T[other, r, :]
        if emit is not None:
            emit(base)


def to_rows(block):
    vectors = block.shape[0]
    return block.reshape(vectors, 3, ROWS, 128).transpose(1, 2, 0, 3)


def from_rows(block):
    vectors = block.shape[2]
    return block.transpose(2, 0, 1, 3).reshape(vectors, 3, ROWS * 128)


def local(orbitals, sign_vectors, potential, cheb_coefs):
    f32 = jnp.float32
    vmem = pl.BlockSpec(memory_space=pltpu.VMEM)
    anywhere = pl.BlockSpec(memory_space=pl.ANY)
    quarter_lanes = 18 * 128
    share = lax.dynamic_slice_in_dim(
        potential, (lax.axis_index("band") % 4) * quarter_lanes, quarter_lanes, 1
    )
    share = jnp.pad(share.reshape(54, 128), ((0, SHARE - 54), (0, 0)))
    field = pltpu.VMEM((NG * XS, 128), f32)
    dma = pltpu.SemaphoreType.DMA
    noise, margins, density = pl.pallas_call(
        everything,
        out_shape=(
            jax.ShapeDtypeStruct((3, ROWS, 8, 128), f32),
            jax.ShapeDtypeStruct((8, 128), f32),
            jax.ShapeDtypeStruct((3, CHUNK * 128), f32),
        ),
        in_specs=[anywhere, anywhere] + [vmem] * 4 + [pl.BlockSpec(memory_space=pltpu.SMEM)],
        out_specs=(vmem, vmem, vmem),
        scratch_shapes=[
            pltpu.VMEM((NG, ROWS, 128), f32),
            pltpu.VMEM((NG, ROWS, 128), jnp.int32),
            pltpu.VMEM((2, NG * XS, 128), f32),
            field, field, field,
            pltpu.VMEM((8 * BLOCK, 128), f32),
            pltpu.VMEM((3, CHUNK, 32, 128), f32),
            pltpu.VMEM((3, CHUNK, 64, 128), jnp.int32),
            pltpu.VMEM((64, 128), f32),
            pltpu.VMEM((64, 128), f32),
            pltpu.VMEM((8, 128), f32),
            pltpu.VMEM((256, 128), f32),
            pltpu.VMEM((8, 128), f32),
            pltpu.VMEM((64, 128), f32),
            pltpu.VMEM((3, ROWS, 4, 128), f32),
            pltpu.VMEM((3, CHUNK, 32, 128), f32),
            pltpu.VMEM((3, CHUNK, 64, 128), f32),
            pltpu.VMEM((3, ROWS, 8, 128), f32),
            pltpu.VMEM((3, ROWS, 8, 128), f32),
            pltpu.VMEM((BANDS, 3 * CHUNK, 128), f32),
            pltpu.VMEM((BANDS, 3 * CHUNK, 128), f32),
            dma((12,)), dma((16,)), dma, dma, dma, dma, dma, dma, dma,
            dma, dma, dma, dma, dma, dma, dma, dma, dma, dma,
            dma, dma, dma, dma, dma, dma, dma, dma, dma,
        ],
        compiler_params=pltpu.CompilerParams(
            vmem_limit_bytes=60 * 2**20, has_side_effects=True, collective_id=1
        ),
    )(
        to_rows(orbitals), to_rows(sign_vectors), share,
        *[jnp.asarray(t) for t in tables()], cheb_coefs,
    )
    return density, margins[:, :32].T, from_rows(noise)


def solution(mesh):
    return jax.shard_map(
        local,
        mesh=mesh,
        in_specs=(P("band", "grid", None), P("band", "grid", None), P("grid", None), P()),
        out_specs=(P("grid", "band"), P(None, "band"), P("band", "grid", None)),
        check_vma=False,
    )
```

```python
import math

import jax
import jax.numpy as jnp
import ml_dtypes
import numpy as np
from jax import lax
from jax.experimental import pallas as pl
from jax.experimental.pallas import tpu as pltpu
from jax.sharding import PartitionSpec as P

NG = 96
ORDER = 6
ROWS = 72
XS = 104
UX, UY, UR = 24, 12, 8
SHARE = 56
BLOCK = 16 * SHARE
BANDS = 8
CHUNK = ROWS // BANDS
SCALE = math.sqrt(float(NG) ** 3)
MESH = pl.DeviceIdType.MESH
ORB_OWNER = tuple(8 * i + 2 * (1 - i % 2) for i in range(4))
STO_OWNER = tuple(4 * s + 2 * ((s // 2) % 2) for s in range(8))


def tables():
    index = np.arange(NG)
    phase = 2.0 * np.pi / NG * ((index[:, None] * index[None, :]) % NG)
    hartley = (np.cos(phase) + np.sin(phase)) / math.sqrt(NG)
    wave = np.minimum(index, NG - index) / (NG / 2.0)
    doubled = 2.0 * (hartley @ (((wave * wave - 0.5) / 3.0)[:, None] * hartley))
    high = doubled.astype(ml_dtypes.bfloat16)
    low = (doubled - high.astype(np.float64)).astype(ml_dtypes.bfloat16)

    def left(order):
        h, l = high[order][:, order], low[order][:, order]
        return np.block([[h, h], [l, l]])

    right = np.zeros((256, 256), ml_dtypes.bfloat16)
    for at in (0, 128):
        right[at : at + NG, 0:NG] = high
        right[at : at + NG, 128 : 128 + NG] = low
    y_order = np.array([4 * (q % 24) + q // 24 for q in range(NG)])
    return left(index), left(y_order), right


def halves(t):
    high = t.astype(jnp.bfloat16)
    return high, (t - high.astype(jnp.float32)).astype(jnp.bfloat16)


def left_mul(matrix, a, b):
    right = jnp.concatenate(
        [jnp.concatenate([a[0], b[0]], 1), jnp.concatenate([a[1], b[1]], 1)], 0
    )
    out = jnp.dot(matrix, right, preferred_element_type=jnp.float32)
    out = out[:NG] + out[NG:]
    return out[:, :128], out[:, 128:]


def spread(a, lane):
    zero = jnp.zeros(lane.shape, jnp.float32)
    one = jnp.where(lane < 32, pltpu.roll(a[0], 32, 1), pltpu.roll(a[1], 32, 1))
    two = jnp.where(lane < 64, pltpu.roll(a[1], 64, 1), pltpu.roll(a[2], 64, 1))
    parts = (a[0], one, two, pltpu.roll(a[2], 96, 1))
    return [jnp.where(lane < 96, part, zero) for part in parts]


def pack(b, lane):
    one = pltpu.roll(b[1], 96, 1)
    two = pltpu.roll(b[2], 64, 1)
    return (
        jnp.where(lane < 96, b[0], one),
        jnp.where(lane < 64, one, two),
        jnp.where(lane < 32, two, pltpu.roll(b[3], 32, 1)),
    )


def quarter(x, j):
    return pl.ds(pl.multiple_of(x * XS + 24 * j, 8), 24)


def wait(view, sem):
    pltpu.make_async_copy(view, view, sem).wait()


def remote(src, dst, send, recv, device):
    return pltpu.make_async_remote_copy(
        src_ref=src, dst_ref=dst, send_sem=send, recv_sem=recv, device_id=device, device_id_type=MESH
    )


def concat_rows(ref, p, kind):
    return jnp.concatenate([ref[p, r].astype(jnp.float32).astype(kind) for r in range(CHUNK)], 1)


def against(a, b, contract):
    return lax.dot_general(a, b, (((1,), (contract,)), ((), ())), preferred_element_type=jnp.float32)


def everything(
    orb, sto, potc, kx, ky, wz, coef_ref, sto_out, mar_out, den_out,
    land, landi, T, W, FI, PO, pot2, a_orb, a_sto, mt, rs, own_sum, gs, own_mar, ms,
    orb_home, a_f, cbuf, c_home, sto_home, sq, sq_in,
    in_sems, pot1_send, pot1_recv, pot2_send, pot2_recv, pot3_send, pot3_recv, land_sem, landi_sem,
    ao_send, ao_recv, as_send, as_recv, rs_send, rs_recv, gs_send, gs_recv, ms_send, ms_recv,
    out_send, oh_recv, sh_recv, af_send, af_recv, c_send, c_recv, sq_send, sq_recv,
):
    me = lax.axis_index("grid")
    band = lax.axis_index("band")
    level = me // 4
    seat = me % 4
    f32 = jnp.float32

    barrier = pltpu.get_barrier_semaphore()
    for j in range(1, 32):
        pl.semaphore_signal(barrier, inc=1, device_id={"grid": lax.rem(me + j, 32)}, device_id_type=MESH)
    for j in range(1, BANDS):
        pl.semaphore_signal(barrier, inc=1, device_id={"band": lax.rem(band + j, BANDS)}, device_id_type=MESH)
    pl.semaphore_wait(barrier, 38)

    turned = (level // 2) % 2
    row = seat // 2
    core = seat % 2
    column = band % 4
    is_chip = jnp.logical_or(row == turned, level % 2 == 0)
    is_sto = jnp.logical_and(core == 0, row == turned)
    is_orb = jnp.logical_and(core == 0, jnp.logical_and(row != turned, level % 2 == 0))
    is_owner = jnp.logical_or(is_sto, is_orb)

    def block(a_core, a_column, blocks=1):
        return pot2.at[pl.ds(pl.multiple_of(BLOCK * (4 * a_core + a_column), 8), BLOCK * blocks)]

    slot = pot2.at[pl.ds(pl.multiple_of(BLOCK * (4 * core + column) + SHARE * (2 * level + row), 8), SHARE)]

    def share(kind, d):
        there = lax.rem(level + d, 8)
        row_to = (there // 2 + kind) % 2
        return remote(
            potc, slot, pot1_send.at[8 * kind + d], pot1_recv, {"grid": there * 4 + 2 * row_to + core}
        )

    def shares(kind, d):
        go = level >= 0 if kind == 0 else (level + d) % 2 == 0
        if d == 0:
            go = jnp.logical_and(go, row != turned if kind == 0 else row == turned)
        return go

    @pl.when(is_chip)
    def _():
        pltpu.make_async_copy(potc, slot, pot1_recv).start()

    for d in range(8):
        for kind in range(2):
            @pl.when(shares(kind, d))
            def _():
                share(kind, d).start()

    def to_owner(v):
        if v < 4:
            return remote(
                orb.at[:, :, v, :], land.at[pl.ds(3 * me, 3)], in_sems.at[v], land_sem, {"grid": ORB_OWNER[v]}
            )
        return remote(
            sto.at[:, :, v - 4, :], landi.at[pl.ds(3 * me, 3)], in_sems.at[v], landi_sem, {"grid": STO_OWNER[v - 4]}
        )

    def send_vectors(low, high):
        for v in range(low, high):
            target = (ORB_OWNER + STO_OWNER)[v]

            @pl.when(me != target)
            def _():
                to_owner(v).start()

            @pl.when(me == target)
            def _():
                if v < 4:
                    pltpu.make_async_copy(orb.at[:, :, v, :], land.at[pl.ds(3 * me, 3)], land_sem).start()
                else:
                    pltpu.make_async_copy(sto.at[:, :, v - 4, :], landi.at[pl.ds(3 * me, 3)], landi_sem).start()

    send_vectors(0, 4)

    def along(d):
        return remote(
            block(core, column), block(core, column), pot2_send, pot2_recv.at[d],
            {"band": (band // 4) * 4 + lax.rem(column + d, 4)},
        )

    hands_over = jnp.logical_and(is_chip, core == 1)

    def across(d):
        from_column = lax.rem(column + 4 - d, 4)
        return remote(
            block(1, from_column), block(1, from_column), pot3_send.at[d], pot3_recv, {"grid": level * 4 + 2 * row}
        )

    @pl.when(is_chip)
    def _():
        wait(block(core, column), pot1_recv)
        for d in range(1, 4):
            along(d).start()

        @pl.when(core == 1)
        def _():
            across(0).start()

    send_vectors(4, 12)

    @pl.when(hands_over)
    def _():
        for d in (1, 3, 2):
            wait(block(0, 0), pot2_recv.at[d])
            across(d).start()

    for v, target in enumerate(ORB_OWNER + STO_OWNER):
        @pl.when(me != target)
        def _():
            to_owner(v).wait_send()

    def cells(src, dst, count, to, sends, recvs):
        return remote(
            src.at[:, pl.ds(CHUNK * to, CHUNK)], dst.at[:, :, pl.ds(pl.multiple_of(count * band, count), count), :],
            sends, recvs, {"band": to},
        )

    def own_cells(src, dst, count, recvs):
        pltpu.make_async_copy(
            src.at[:, pl.ds(CHUNK * band, CHUNK)],
            dst.at[:, :, pl.ds(pl.multiple_of(count * band, count), count), :], recvs,
        ).start()

    own_cells(orb, a_orb, 4, ao_recv)
    own_cells(sto, a_sto, 8, as_recv)
    for d in range(1, 8):
        to = lax.rem(band + d, BANDS)
        cells(orb, a_orb, 4, to, ao_send, ao_recv).start()
        cells(sto, a_sto, 8, to, as_send, as_recv).start()

    def eight(ref, at):
        return ref.at[pl.ds(pl.multiple_of(8 * at, 8), 8)]

    def service_partial():
        wait(a_orb, ao_recv)
        wait(a_sto, as_recv)
        total = jnp.zeros((64, 32), f32)
        for p in range(3):
            signs = concat_rows(a_sto, p, jnp.bfloat16)
            for part in halves(concat_rows(a_orb, p, f32)):
                total += against(signs, part, 1)
        mt[...] = jnp.zeros((64, 128), f32)
        mt[:, 0:32] = total
        pltpu.make_async_copy(eight(mt, band), eight(rs, band), rs_recv).start()
        for d in range(1, 8):
            to = lax.rem(band + d, BANDS)
            remote(eight(mt, to), eight(rs, band), rs_send, rs_recv, {"band": to}).start()

    def service_slab():
        wait(rs, rs_recv)
        own_sum[...] = sum(rs[8 * j : 8 * j + 8, :] for j in range(8))
        pltpu.make_async_copy(own_sum, eight(gs, me), gs_recv).start()

        @pl.loop(1, 32)
        def _(d):
            remote(own_sum, eight(gs, me), gs_send, gs_recv, {"grid": lax.rem(me + d, 32)}).start()

    def service_whole():
        wait(gs, gs_recv)
        margins = sum(gs[8 * j : 8 * j + 8, :] for j in range(32)) / SCALE
        own_mar[...] = margins
        mar_out[...] = margins
        pltpu.make_async_copy(own_mar, eight(ms, band), ms_recv).start()
        for d in range(1, 8):
            remote(own_mar, eight(ms, band), ms_send, ms_recv, {"band": lax.rem(band + d, BANDS)}).start()

    @pl.when(jnp.logical_not(is_owner))
    def _():
        service_partial()
        service_slab()

    def forward_orbitals():
        wait(orb_home, oh_recv)
        own_cells(orb_home, a_f, 4, af_recv)
        for d in range(1, 8):
            cells(orb_home, a_f, 4, lax.rem(band + d, BANDS), af_send, af_recv).start()

    @pl.when(is_owner)
    def _():
        for d in range(1, 4):
            wait(block(0, 0), pot2_recv.at[d])
        wait(block(0, 0, 4), pot3_recv)
        small = lax.broadcasted_iota(jnp.int32, (16, 128), 1)

        @pl.loop(0, 8)
        def _(q):
            for p in range(3):
                for m in range(6):
                    parts = spread(
                        [pot2[pl.ds(q * BLOCK + p * 18 + 3 * m + k, 16, stride=SHARE), :] for k in range(3)], small
                    )
                    for j, part in enumerate(parts):
                        at = (3 * (q // 4) + p) * XS + 24 * j + 6 * (q % 4) + m
                        PO[pl.ds(at, 16, stride=6 * XS), :] = 2.0 * part

        lane = lax.broadcasted_iota(jnp.int32, (24, 128), 1)

        last_coef = coef_ref[ORDER]

        def take(source):
            @pl.loop(0, NG, step=UR)
            def _(base):
                for u in range(UR):
                    x = base + u
                    rows = [source[x, pl.ds(k, 24, stride=3), :].astype(f32) for k in range(3)]
                    for j, part in enumerate(spread(rows, lane)):
                        T[0, quarter(x, j), :] = last_coef * part
                        FI[quarter(x, j), :] = part

        @pl.when(is_orb)
        def _():
            wait(land, land_sem)
            take(land)

        @pl.when(is_sto)
        def _():
            wait(landi, landi_sem)
            take(landi)

        fields = (kx, ky, wz, coef_ref, T, W, FI, PO)
        apply_operator(0, 0, 1, UY, None, *fields)

        @pl.loop(1, ORDER - 1)
        def _(k):
            @pl.when(jnp.logical_and(is_sto, k == ORDER - 2))
            def _():
                service_partial()

            apply_operator(k, lax.rem(k, 2), 1 - lax.rem(k, 2), UY, None, *fields)

        @pl.when(is_sto)
        def _():
            service_slab()

        def give(to, home, at, recv):
            slab = land.at[pl.ds(3 * to, 3)]

            @pl.when(to != me)
            def _():
                remote(slab, home.at[:, :, at, :], out_send, recv, {"grid": to}).start()

            @pl.when(to == me)
            def _():
                pltpu.make_async_copy(slab, home.at[:, :, at, :], recv).start()

        def hand_back(base):
            for u in range(12):
                x = base + u
                for k, part in enumerate(pack([FI[quarter(x, j), :] for j in range(4)], lane)):
                    land[x, pl.ds(k, 24, stride=3), :] = part
            @pl.when(is_orb)
            def _():
                for u in range(4):
                    give(base // 3 + u, orb_home, level // 2, oh_recv)

        apply_operator(ORDER - 1, 1, 0, 6, hand_back, *fields)

        @pl.when(is_orb)
        def _():
            service_partial()
            service_slab()

        @pl.when(is_sto)
        def _():
            service_whole()
            forward_orbitals()

            @pl.loop(0, 32)
            def _(d):
                give(lax.rem(me + d, 32), sto_home, level, sh_recv)

    @pl.when(jnp.logical_not(is_sto))
    def _():
        service_whole()
        forward_orbitals()

    wait(ms, ms_recv)
    m_high, m_low = halves(ms[:, 0:32] * (1.0 / SCALE))
    wait(a_f, af_recv)
    orb_squares = []
    for p in range(3):
        field = concat_rows(a_f, p, f32)
        f_high, f_low = halves(field)
        change = against(m_high, f_high, 0) + against(m_high, f_low, 0) + against(m_low, f_high, 0)
        summed = jnp.sum(field * field, axis=0, keepdims=True)
        for r in range(CHUNK):
            cbuf[p, r] = change[:, 128 * r : 128 * r + 128]
            orb_squares.append(summed[:, 128 * r : 128 * r + 128])

    def back(to):
        return remote(
            cbuf.at[:, :, pl.ds(pl.multiple_of(8 * to, 8), 8), :], c_home.at[:, pl.ds(CHUNK * band, CHUNK)],
            c_send, c_recv, {"band": to},
        )

    pltpu.make_async_copy(
        cbuf.at[:, :, pl.ds(pl.multiple_of(8 * band, 8), 8), :], c_home.at[:, pl.ds(CHUNK * band, CHUNK)], c_recv
    ).start()
    for d in range(1, 8):
        back(lax.rem(band + d, BANDS)).start()

    wait(c_home, c_recv)
    wait(sto_home, sh_recv)

    @pl.loop(0, BANDS)
    def _(b):
        for p in range(3):
            for r in range(CHUNK):
                at = b * CHUNK + r
                value = sto_home[p, at] - c_home[p, at]
                sto_out[p, at] = value
                sq[b, pl.ds(p * CHUNK + r, 1), :] = jnp.sum(value * value, axis=0, keepdims=True)

    pltpu.make_async_copy(sq.at[band], sq_in.at[band], sq_recv).start()
    for d in range(1, 8):
        to = lax.rem(band + d, BANDS)
        remote(sq.at[to], sq_in.at[band], sq_send, sq_recv, {"band": to}).start()
    wait(sq_in, sq_recv)
    noise_part = sum(sq_in[b] for b in range(BANDS))
    for p in range(3):
        for r in range(CHUNK):
            at = p * CHUNK + r
            den_out[p : p + 1, 128 * r : 128 * r + 128] = (orb_squares[at] + noise_part[at : at + 1]) / 96.0

    for d in range(8):
        for kind in range(2):
            @pl.when(shares(kind, d))
            def _():
                share(kind, d).wait_send()

    @pl.when(is_chip)
    def _():
        wait(block(0, 0, 3), pot2_send)

        @pl.when(hands_over)
        def _():
            for d in range(4):
                across(d).wait_send()

    wait(orb.at[:, pl.ds(0, 7 * CHUNK)], ao_send)
    wait(sto.at[:, pl.ds(0, 7 * CHUNK)], as_send)
    wait(rs.at[pl.ds(0, 56)], rs_send)
    wait(gs.at[pl.ds(0, 248)], gs_send)
    wait(ms.at[pl.ds(0, 56)], ms_send)

    @pl.when(is_owner)
    def _():
        wait(land.at[pl.ds(0, 93)], out_send)

    wait(orb_home.at[:, pl.ds(0, 7 * CHUNK)], af_send)
    wait(c_home.at[:, pl.ds(0, 7 * CHUNK)], c_send)
    wait(sq.at[pl.ds(0, 7)], sq_send)


def apply_operator(k, now, other, group, emit, kx_ref, ky_ref, wz_ref, coef_ref, T, W, FI, PO):
    coef = coef_ref[ORDER - 1 - k]

    @pl.loop(0, NG, step=2 * UX)
    def _(base):
        for u in range(UX):
            y = base + 2 * u
            columns = [pl.ds(y + q, NG, stride=XS) for q in range(2)]
            outs = left_mul(kx_ref[...], *[halves(T[now, c, :]) for c in columns])
            for c, out in zip(columns, outs):
                W[c, :] = out

    @pl.loop(0, NG, step=2 * group)
    def _(base):
        rows = [pl.ds(pl.multiple_of((base + q) * XS, 8), NG) for q in range(2 * group)]
        held = [T[now, r, :] for r in rows]
        split = [halves(t) for t in held]
        for u in range(group):
            along_y = left_mul(ky_ref[...], split[2 * u], split[2 * u + 1])
            stacked = jnp.concatenate([jnp.concatenate(split[2 * u + q], 1) for q in range(2)], 0)
            along_z = jnp.dot(stacked, wz_ref[...], preferred_element_type=jnp.float32)
            for q in range(2):
                r = rows[2 * u + q]
                t = held[2 * u + q]
                z = along_z[NG * q : NG * (q + 1)]
                total = z[:, :128] + z[:, 128:] + along_y[q] + W[r, :] + PO[r, :] * t
                if emit is not None:
                    FI[r, :] = coef * FI[r, :] + 0.5 * total - T[other, r, :]
                elif isinstance(k, int):
                    T[other, r, :] = coef * FI[r, :] + total
                else:
                    T[other, r, :] = coef * FI[r, :] + total - T[other, r, :]
        if emit is not None:
            emit(base)


def to_rows(block):
    vectors = block.shape[0]
    return block.reshape(vectors, 3, ROWS, 128).transpose(1, 2, 0, 3)


def from_rows(block):
    vectors = block.shape[2]
    return block.transpose(2, 0, 1, 3).reshape(vectors, 3, ROWS * 128)


def local(orbitals, sign_vectors, potential, cheb_coefs):
    f32 = jnp.float32
    vmem = pl.BlockSpec(memory_space=pltpu.VMEM)
    anywhere = pl.BlockSpec(memory_space=pl.ANY)
    quarter_lanes = 18 * 128
    share = lax.dynamic_slice_in_dim(
        potential, (lax.axis_index("band") % 4) * quarter_lanes, quarter_lanes, 1
    )
    share = jnp.pad(share.reshape(54, 128), ((0, SHARE - 54), (0, 0)))
    field = pltpu.VMEM((NG * XS, 128), f32)
    dma = pltpu.SemaphoreType.DMA
    noise, margins, density = pl.pallas_call(
        everything,
        out_shape=(
            jax.ShapeDtypeStruct((3, ROWS, 8, 128), f32),
            jax.ShapeDtypeStruct((8, 128), f32),
            jax.ShapeDtypeStruct((3, CHUNK * 128), f32),
        ),
        in_specs=[anywhere, anywhere] + [vmem] * 4 + [pl.BlockSpec(memory_space=pltpu.SMEM)],
        out_specs=(vmem, vmem, vmem),
        scratch_shapes=[
            pltpu.VMEM((NG, ROWS, 128), f32),
            pltpu.VMEM((NG, ROWS, 128), jnp.int32),
            pltpu.VMEM((2, NG * XS, 128), f32),
            field, field, field,
            pltpu.VMEM((8 * BLOCK, 128), f32),
            pltpu.VMEM((3, CHUNK, 32, 128), f32),
            pltpu.VMEM((3, CHUNK, 64, 128), jnp.int32),
            pltpu.VMEM((64, 128), f32),
            pltpu.VMEM((64, 128), f32),
            pltpu.VMEM((8, 128), f32),
            pltpu.VMEM((256, 128), f32),
            pltpu.VMEM((8, 128), f32),
            pltpu.VMEM((64, 128), f32),
            pltpu.VMEM((3, ROWS, 4, 128), f32),
            pltpu.VMEM((3, CHUNK, 32, 128), f32),
            pltpu.VMEM((3, CHUNK, 64, 128), f32),
            pltpu.VMEM((3, ROWS, 8, 128), f32),
            pltpu.VMEM((3, ROWS, 8, 128), f32),
            pltpu.VMEM((BANDS, 3 * CHUNK, 128), f32),
            pltpu.VMEM((BANDS, 3 * CHUNK, 128), f32),
            dma((12,)), dma((16,)), dma, dma, dma((4,)), dma((4,)), dma, dma, dma,
            dma, dma, dma, dma, dma, dma, dma, dma, dma, dma,
            dma, dma, dma, dma, dma, dma, dma, dma, dma,
        ],
        compiler_params=pltpu.CompilerParams(
            vmem_limit_bytes=60 * 2**20, has_side_effects=True, collective_id=1
        ),
    )(
        to_rows(orbitals), to_rows(sign_vectors), share,
        *[jnp.asarray(t) for t in tables()], cheb_coefs,
    )
    return density, margins[:, :32].T, from_rows(noise)


def solution(mesh):
    return jax.shard_map(
        local,
        mesh=mesh,
        in_specs=(P("band", "grid", None), P("band", "grid", None), P("grid", None), P()),
        out_specs=(P("grid", "band"), P(None, "band"), P("band", "grid", None)),
        check_vma=False,
    )
```

```python
import math

import jax
import jax.numpy as jnp
import ml_dtypes
import numpy as np
from jax import lax
from jax.experimental import pallas as pl
from jax.experimental.pallas import tpu as pltpu
from jax.sharding import PartitionSpec as P

NG = 96
ORDER = 6
ROWS = 72
XS = 104
UX, UY, UR = 24, 12, 8
SHARE = 56
BLOCK = 16 * SHARE
BANDS = 8
CHUNK = ROWS // BANDS
SCALE = math.sqrt(float(NG) ** 3)
MESH = pl.DeviceIdType.MESH
ORB_OWNER = tuple(8 * i + 2 * (1 - i % 2) for i in range(4))
STO_OWNER = tuple(4 * s + 2 * ((s // 2) % 2) for s in range(8))


def tables():
    index = np.arange(NG)
    phase = 2.0 * np.pi / NG * ((index[:, None] * index[None, :]) % NG)
    hartley = (np.cos(phase) + np.sin(phase)) / math.sqrt(NG)
    wave = np.minimum(index, NG - index) / (NG / 2.0)
    doubled = 2.0 * (hartley @ (((wave * wave - 0.5) / 3.0)[:, None] * hartley))
    high = doubled.astype(ml_dtypes.bfloat16)
    low = (doubled - high.astype(np.float64)).astype(ml_dtypes.bfloat16)

    def left(order):
        h, l = high[order][:, order], low[order][:, order]
        return np.block([[h, h], [l, l]])

    right = np.zeros((256, 256), ml_dtypes.bfloat16)
    for at in (0, 128):
        right[at : at + NG, 0:NG] = high
        right[at : at + NG, 128 : 128 + NG] = low
    y_order = np.array([4 * (q % 24) + q // 24 for q in range(NG)])
    return left(index), left(y_order), right


def halves(t):
    high = t.astype(jnp.bfloat16)
    return high, (t - high.astype(jnp.float32)).astype(jnp.bfloat16)


def left_mul(matrix, a, b):
    right = jnp.concatenate(
        [jnp.concatenate([a[0], b[0]], 1), jnp.concatenate([a[1], b[1]], 1)], 0
    )
    out = jnp.dot(matrix, right, preferred_element_type=jnp.float32)
    out = out[:NG] + out[NG:]
    return out[:, :128], out[:, 128:]


def spread(a, lane):
    zero = jnp.zeros(lane.shape, jnp.float32)
    one = jnp.where(lane < 32, pltpu.roll(a[0], 32, 1), pltpu.roll(a[1], 32, 1))
    two = jnp.where(lane < 64, pltpu.roll(a[1], 64, 1), pltpu.roll(a[2], 64, 1))
    parts = (a[0], one, two, pltpu.roll(a[2], 96, 1))
    return [jnp.where(lane < 96, part, zero) for part in parts]


def pack(b, lane):
    one = pltpu.roll(b[1], 96, 1)
    two = pltpu.roll(b[2], 64, 1)
    return (
        jnp.where(lane < 96, b[0], one),
        jnp.where(lane < 64, one, two),
        jnp.where(lane < 32, two, pltpu.roll(b[3], 32, 1)),
    )


def quarter(x, j):
    return pl.ds(pl.multiple_of(x * XS + 24 * j, 8), 24)


def wait(view, sem):
    pltpu.make_async_copy(view, view, sem).wait()


def remote(src, dst, send, recv, device):
    return pltpu.make_async_remote_copy(
        src_ref=src, dst_ref=dst, send_sem=send, recv_sem=recv, device_id=device, device_id_type=MESH
    )


def concat_rows(ref, p, kind):
    return jnp.concatenate([ref[p, r].astype(jnp.float32).astype(kind) for r in range(CHUNK)], 1)


def against(a, b, contract):
    return lax.dot_general(a, b, (((1,), (contract,)), ((), ())), preferred_element_type=jnp.float32)


def everything(
    orb, sto, potc, kx, ky, wz, coef_ref, sto_out, mar_out, den_out,
    land, landi, T, W, FI, PO, pot2, a_orb, a_sto, mt, rs, own_sum, gs, own_mar, ms,
    orb_home, a_f, cbuf, c_home, sto_home, sq, sq_in,
    in_sems, pot1_send, pot1_recv, pot2_send, pot2_recv, pot3_send, pot3_recv, land_sem, landi_sem,
    ao_send, ao_recv, as_send, as_recv, rs_send, rs_recv, gs_send, gs_recv, ms_send, ms_recv,
    out_send, oh_recv, sh_recv, af_send, af_recv, c_send, c_recv, sq_send, sq_recv,
):
    me = lax.axis_index("grid")
    band = lax.axis_index("band")
    level = me // 4
    seat = me % 4
    f32 = jnp.float32

    barrier = pltpu.get_barrier_semaphore()
    for j in range(1, 32):
        pl.semaphore_signal(barrier, inc=1, device_id={"grid": lax.rem(me + j, 32)}, device_id_type=MESH)
    for j in range(1, BANDS):
        pl.semaphore_signal(barrier, inc=1, device_id={"band": lax.rem(band + j, BANDS)}, device_id_type=MESH)
    pl.semaphore_wait(barrier, 38)

    turned = (level // 2) % 2
    row = seat // 2
    core = seat % 2
    column = band % 4
    is_chip = jnp.logical_or(row == turned, level % 2 == 0)
    is_sto = jnp.logical_and(core == 0, row == turned)
    is_orb = jnp.logical_and(core == 0, jnp.logical_and(row != turned, level % 2 == 0))
    is_owner = jnp.logical_or(is_sto, is_orb)

    def block(a_core, a_column, blocks=1):
        return pot2.at[pl.ds(pl.multiple_of(BLOCK * (4 * a_core + a_column), 8), BLOCK * blocks)]

    slot = pot2.at[pl.ds(pl.multiple_of(BLOCK * (4 * core + column) + SHARE * (2 * level + row), 8), SHARE)]

    def share(kind, d):
        there = lax.rem(level + d, 8)
        row_to = (there // 2 + kind) % 2
        return remote(
            potc, slot, pot1_send.at[8 * kind + d], pot1_recv, {"grid": there * 4 + 2 * row_to + core}
        )

    def shares(kind, d):
        go = level >= 0 if kind == 0 else (level + d) % 2 == 0
        if d == 0:
            go = jnp.logical_and(go, row != turned if kind == 0 else row == turned)
        return go

    @pl.when(is_chip)
    def _():
        pltpu.make_async_copy(potc, slot, pot1_recv).start()

    for d in range(8):
        for kind in range(2):
            @pl.when(shares(kind, d))
            def _():
                share(kind, d).start()

    def to_owner(v):
        if v < 4:
            return remote(
                orb.at[:, :, v, :], land.at[pl.ds(3 * me, 3)], in_sems.at[v], land_sem, {"grid": ORB_OWNER[v]}
            )
        return remote(
            sto.at[:, :, v - 4, :], landi.at[pl.ds(3 * me, 3)], in_sems.at[v], landi_sem, {"grid": STO_OWNER[v - 4]}
        )

    def send_vectors(low, high):
        for v in range(low, high):
            target = (ORB_OWNER + STO_OWNER)[v]

            @pl.when(me != target)
            def _():
                to_owner(v).start()

            @pl.when(me == target)
            def _():
                if v < 4:
                    pltpu.make_async_copy(orb.at[:, :, v, :], land.at[pl.ds(3 * me, 3)], land_sem).start()
                else:
                    pltpu.make_async_copy(sto.at[:, :, v - 4, :], landi.at[pl.ds(3 * me, 3)], landi_sem).start()

    send_vectors(0, 4)

    def along(d):
        return remote(
            block(core, column), block(core, column), pot2_send, pot2_recv.at[d],
            {"band": (band // 4) * 4 + lax.rem(column + d, 4)},
        )

    hands_over = jnp.logical_and(is_chip, core == 1)

    def across(d):
        from_column = lax.rem(column + 4 - d, 4)
        return remote(
            block(1, from_column), block(1, from_column), pot3_send.at[d], pot3_recv, {"grid": level * 4 + 2 * row}
        )

    @pl.when(is_chip)
    def _():
        wait(block(core, column), pot1_recv)
        for d in range(1, 4):
            along(d).start()

        @pl.when(core == 1)
        def _():
            across(0).start()

    send_vectors(4, 12)

    @pl.when(hands_over)
    def _():
        for d in (1, 3, 2):
            wait(block(0, 0), pot2_recv.at[d])
            across(d).start()

    for v, target in enumerate(ORB_OWNER + STO_OWNER):
        @pl.when(me != target)
        def _():
            to_owner(v).wait_send()

    def cells(src, dst, count, to, sends, recvs):
        return remote(
            src.at[:, pl.ds(CHUNK * to, CHUNK)], dst.at[:, :, pl.ds(pl.multiple_of(count * band, count), count), :],
            sends, recvs, {"band": to},
        )

    def own_cells(src, dst, count, recvs):
        pltpu.make_async_copy(
            src.at[:, pl.ds(CHUNK * band, CHUNK)],
            dst.at[:, :, pl.ds(pl.multiple_of(count * band, count), count), :], recvs,
        ).start()

    own_cells(orb, a_orb, 4, ao_recv)
    own_cells(sto, a_sto, 8, as_recv)
    for d in range(1, 8):
        to = lax.rem(band + d, BANDS)
        cells(orb, a_orb, 4, to, ao_send, ao_recv).start()
        cells(sto, a_sto, 8, to, as_send, as_recv).start()

    def eight(ref, at):
        return ref.at[pl.ds(pl.multiple_of(8 * at, 8), 8)]

    def service_partial():
        wait(a_orb, ao_recv)
        wait(a_sto, as_recv)
        total = jnp.zeros((64, 32), f32)
        for p in range(3):
            signs = concat_rows(a_sto, p, jnp.bfloat16)
            for part in halves(concat_rows(a_orb, p, f32)):
                total += against(signs, part, 1)
        mt[...] = jnp.zeros((64, 128), f32)
        mt[:, 0:32] = total
        pltpu.make_async_copy(eight(mt, band), eight(rs, band), rs_recv).start()
        for d in range(1, 8):
            to = lax.rem(band + d, BANDS)
            remote(eight(mt, to), eight(rs, band), rs_send, rs_recv, {"band": to}).start()

    def service_slab():
        wait(rs, rs_recv)
        own_sum[...] = sum(rs[8 * j : 8 * j + 8, :] for j in range(8))
        pltpu.make_async_copy(own_sum, eight(gs, me), gs_recv).start()

        @pl.loop(1, 32)
        def _(d):
            remote(own_sum, eight(gs, me), gs_send, gs_recv, {"grid": lax.rem(me + d, 32)}).start()

    def service_whole():
        wait(gs, gs_recv)
        margins = sum(gs[8 * j : 8 * j + 8, :] for j in range(32)) / SCALE
        own_mar[...] = margins
        mar_out[...] = margins
        pltpu.make_async_copy(own_mar, eight(ms, band), ms_recv).start()
        for d in range(1, 8):
            remote(own_mar, eight(ms, band), ms_send, ms_recv, {"band": lax.rem(band + d, BANDS)}).start()

    @pl.when(jnp.logical_not(is_owner))
    def _():
        service_partial()
        service_slab()

    @pl.when(is_owner)
    def _():
        for d in range(1, 4):
            wait(block(0, 0), pot2_recv.at[d])
        wait(block(0, 0, 4), pot3_recv)
        small = lax.broadcasted_iota(jnp.int32, (16, 128), 1)

        @pl.loop(0, 8)
        def _(q):
            for p in range(3):
                for m in range(6):
                    parts = spread(
                        [pot2[pl.ds(q * BLOCK + p * 18 + 3 * m + k, 16, stride=SHARE), :] for k in range(3)], small
                    )
                    for j, part in enumerate(parts):
                        at = (3 * (q // 4) + p) * XS + 24 * j + 6 * (q % 4) + m
                        PO[pl.ds(at, 16, stride=6 * XS), :] = 2.0 * part

        lane = lax.broadcasted_iota(jnp.int32, (24, 128), 1)

        last_coef = coef_ref[ORDER]

        def take(source):
            @pl.loop(0, NG, step=UR)
            def _(base):
                for u in range(UR):
                    x = base + u
                    rows = [source[x, pl.ds(k, 24, stride=3), :].astype(f32) for k in range(3)]
                    for j, part in enumerate(spread(rows, lane)):
                        T[0, quarter(x, j), :] = last_coef * part
                        FI[quarter(x, j), :] = part

        @pl.when(is_orb)
        def _():
            wait(land, land_sem)
            take(land)

        @pl.when(is_sto)
        def _():
            wait(landi, landi_sem)
            take(landi)

        fields = (kx, ky, wz, coef_ref, T, W, FI, PO)
        apply_operator(0, 0, 1, UY, None, *fields)

        @pl.loop(1, ORDER - 1)
        def _(k):
            @pl.when(jnp.logical_and(is_sto, k == ORDER - 2))
            def _():
                service_partial()

            apply_operator(k, lax.rem(k, 2), 1 - lax.rem(k, 2), UY, None, *fields)

        @pl.when(is_sto)
        def _():
            service_slab()

        def hand_back(base):
            for u in range(12):
                x = base + u
                for k, part in enumerate(pack([FI[quarter(x, j), :] for j in range(4)], lane)):
                    land[x, pl.ds(k, 24, stride=3), :] = part
            for u in range(4):
                to = base // 3 + u
                slab = land.at[pl.ds(3 * to, 3)]
                for kind, home, at, recv in (
                    (is_orb, orb_home, level // 2, oh_recv), (is_sto, sto_home, level, sh_recv)
                ):
                    @pl.when(jnp.logical_and(kind, to != me))
                    def _():
                        remote(slab, home.at[:, :, at, :], out_send, recv, {"grid": to}).start()

                    @pl.when(jnp.logical_and(kind, to == me))
                    def _():
                        pltpu.make_async_copy(slab, home.at[:, :, at, :], recv).start()

        apply_operator(ORDER - 1, 1, 0, 6, hand_back, *fields)

        @pl.when(is_orb)
        def _():
            service_partial()
            service_slab()

    service_whole()
    wait(orb_home, oh_recv)
    own_cells(orb_home, a_f, 4, af_recv)
    for d in range(1, 8):
        cells(orb_home, a_f, 4, lax.rem(band + d, BANDS), af_send, af_recv).start()
    wait(ms, ms_recv)
    m_high, m_low = halves(ms[:, 0:32] * (1.0 / SCALE))
    wait(a_f, af_recv)
    orb_squares = []
    for p in range(3):
        field = concat_rows(a_f, p, f32)
        f_high, f_low = halves(field)
        change = against(m_high, f_high, 0) + against(m_high, f_low, 0) + against(m_low, f_high, 0)
        summed = jnp.sum(field * field, axis=0, keepdims=True)
        for r in range(CHUNK):
            cbuf[p, r] = change[:, 128 * r : 128 * r + 128]
            orb_squares.append(summed[:, 128 * r : 128 * r + 128])

    def back(to):
        return remote(
            cbuf.at[:, :, pl.ds(pl.multiple_of(8 * to, 8), 8), :], c_home.at[:, pl.ds(CHUNK * band, CHUNK)],
            c_send, c_recv, {"band": to},
        )

    pltpu.make_async_copy(
        cbuf.at[:, :, pl.ds(pl.multiple_of(8 * band, 8), 8), :], c_home.at[:, pl.ds(CHUNK * band, CHUNK)], c_recv
    ).start()
    for d in range(1, 8):
        back(lax.rem(band + d, BANDS)).start()

    wait(c_home, c_recv)
    wait(sto_home, sh_recv)

    @pl.loop(0, BANDS)
    def _(b):
        for p in range(3):
            for r in range(CHUNK):
                at = b * CHUNK + r
                value = sto_home[p, at] - c_home[p, at]
                sto_out[p, at] = value
                sq[b, pl.ds(p * CHUNK + r, 1), :] = jnp.sum(value * value, axis=0, keepdims=True)

    pltpu.make_async_copy(sq.at[band], sq_in.at[band], sq_recv).start()
    for d in range(1, 8):
        to = lax.rem(band + d, BANDS)
        remote(sq.at[to], sq_in.at[band], sq_send, sq_recv, {"band": to}).start()
    wait(sq_in, sq_recv)
    noise_part = sum(sq_in[b] for b in range(BANDS))
    for p in range(3):
        for r in range(CHUNK):
            at = p * CHUNK + r
            den_out[p : p + 1, 128 * r : 128 * r + 128] = (orb_squares[at] + noise_part[at : at + 1]) / 96.0

    for d in range(8):
        for kind in range(2):
            @pl.when(shares(kind, d))
            def _():
                share(kind, d).wait_send()

    @pl.when(is_chip)
    def _():
        wait(block(0, 0, 3), pot2_send)

        @pl.when(hands_over)
        def _():
            for d in range(4):
                across(d).wait_send()

    wait(orb.at[:, pl.ds(0, 7 * CHUNK)], ao_send)
    wait(sto.at[:, pl.ds(0, 7 * CHUNK)], as_send)
    wait(rs.at[pl.ds(0, 56)], rs_send)
    wait(gs.at[pl.ds(0, 248)], gs_send)
    wait(ms.at[pl.ds(0, 56)], ms_send)

    @pl.when(is_owner)
    def _():
        wait(land.at[pl.ds(0, 93)], out_send)

    wait(orb_home.at[:, pl.ds(0, 7 * CHUNK)], af_send)
    wait(c_home.at[:, pl.ds(0, 7 * CHUNK)], c_send)
    wait(sq.at[pl.ds(0, 7)], sq_send)


def apply_operator(k, now, other, group, emit, kx_ref, ky_ref, wz_ref, coef_ref, T, W, FI, PO):
    coef = coef_ref[ORDER - 1 - k]

    @pl.loop(0, NG, step=2 * UX)
    def _(base):
        for u in range(UX):
            y = base + 2 * u
            columns = [pl.ds(y + q, NG, stride=XS) for q in range(2)]
            outs = left_mul(kx_ref[...], *[halves(T[now, c, :]) for c in columns])
            for c, out in zip(columns, outs):
                W[c, :] = out

    @pl.loop(0, NG, step=2 * group)
    def _(base):
        rows = [pl.ds(pl.multiple_of((base + q) * XS, 8), NG) for q in range(2 * group)]
        held = [T[now, r, :] for r in rows]
        split = [halves(t) for t in held]
        for u in range(group):
            along_y = left_mul(ky_ref[...], split[2 * u], split[2 * u + 1])
            stacked = jnp.concatenate([jnp.concatenate(split[2 * u + q], 1) for q in range(2)], 0)
            along_z = jnp.dot(stacked, wz_ref[...], preferred_element_type=jnp.float32)
            for q in range(2):
                r = rows[2 * u + q]
                t = held[2 * u + q]
                z = along_z[NG * q : NG * (q + 1)]
                total = z[:, :128] + z[:, 128:] + along_y[q] + W[r, :] + PO[r, :] * t
                if emit is not None:
                    FI[r, :] = coef * FI[r, :] + 0.5 * total - T[other, r, :]
                elif isinstance(k, int):
                    T[other, r, :] = coef * FI[r, :] + total
                else:
                    T[other, r, :] = coef * FI[r, :] + total - T[other, r, :]
        if emit is not None:
            emit(base)


def to_rows(block):
    vectors = block.shape[0]
    return block.reshape(vectors, 3, ROWS, 128).transpose(1, 2, 0, 3)


def from_rows(block):
    vectors = block.shape[2]
    return block.transpose(2, 0, 1, 3).reshape(vectors, 3, ROWS * 128)


def local(orbitals, sign_vectors, potential, cheb_coefs):
    f32 = jnp.float32
    vmem = pl.BlockSpec(memory_space=pltpu.VMEM)
    anywhere = pl.BlockSpec(memory_space=pl.ANY)
    quarter_lanes = 18 * 128
    share = lax.dynamic_slice_in_dim(
        potential, (lax.axis_index("band") % 4) * quarter_lanes, quarter_lanes, 1
    )
    share = jnp.pad(share.reshape(54, 128), ((0, SHARE - 54), (0, 0)))
    field = pltpu.VMEM((NG * XS, 128), f32)
    dma = pltpu.SemaphoreType.DMA
    noise, margins, density = pl.pallas_call(
        everything,
        out_shape=(
            jax.ShapeDtypeStruct((3, ROWS, 8, 128), f32),
            jax.ShapeDtypeStruct((8, 128), f32),
            jax.ShapeDtypeStruct((3, CHUNK * 128), f32),
        ),
        in_specs=[anywhere, anywhere] + [vmem] * 4 + [pl.BlockSpec(memory_space=pltpu.SMEM)],
        out_specs=(vmem, vmem, vmem),
        scratch_shapes=[
            pltpu.VMEM((NG, ROWS, 128), f32),
            pltpu.VMEM((NG, ROWS, 128), jnp.int32),
            pltpu.VMEM((2, NG * XS, 128), f32),
            field, field, field,
            pltpu.VMEM((8 * BLOCK, 128), f32),
            pltpu.VMEM((3, CHUNK, 32, 128), f32),
            pltpu.VMEM((3, CHUNK, 64, 128), jnp.int32),
            pltpu.VMEM((64, 128), f32),
            pltpu.VMEM((64, 128), f32),
            pltpu.VMEM((8, 128), f32),
            pltpu.VMEM((256, 128), f32),
            pltpu.VMEM((8, 128), f32),
            pltpu.VMEM((64, 128), f32),
            pltpu.VMEM((3, ROWS, 4, 128), f32),
            pltpu.VMEM((3, CHUNK, 32, 128), f32),
            pltpu.VMEM((3, CHUNK, 64, 128), f32),
            pltpu.VMEM((3, ROWS, 8, 128), f32),
            pltpu.VMEM((3, ROWS, 8, 128), f32),
            pltpu.VMEM((BANDS, 3 * CHUNK, 128), f32),
            pltpu.VMEM((BANDS, 3 * CHUNK, 128), f32),
            dma((12,)), dma((16,)), dma, dma, dma((4,)), dma((4,)), dma, dma, dma,
            dma, dma, dma, dma, dma, dma, dma, dma, dma, dma,
            dma, dma, dma, dma, dma, dma, dma, dma, dma,
        ],
        compiler_params=pltpu.CompilerParams(
            vmem_limit_bytes=60 * 2**20, has_side_effects=True, collective_id=1
        ),
    )(
        to_rows(orbitals), to_rows(sign_vectors), share,
        *[jnp.asarray(t) for t in tables()], cheb_coefs,
    )
    return density, margins[:, :32].T, from_rows(noise)


def solution(mesh):
    return jax.shard_map(
        local,
        mesh=mesh,
        in_specs=(P("band", "grid", None), P("band", "grid", None), P("grid", None), P()),
        out_specs=(P("grid", "band"), P(None, "band"), P("band", "grid", None)),
        check_vma=False,
    )
```
